512 devices in a mesh: gx: 16 (over z), gy: 8 (over y, core), gz: 4 (over x).
Axes of the slice: x: 4, y: 4, z: 16, core: 2. Of those that a mesh axis runs over, the one named last changes fastest.
Arguments:
- prior_thermal_state: float32 [128, 128, 512], P('gx', 'gy', 'gz'), may hold values from -6 to 6
- diffusivity_root_factor: float32 [128, 128, 512], P('gx', 'gy', 'gz'), may hold values from 0.5 to 1.5
- bead_strip_energy: float32 [32768, 512], P(('gx', 'gy'), 'gz'), may hold values from -6 to 6
- holding_tile_ordinal: int32 [32768, 1], P(('gx', 'gy')), may hold values from 0 to 127; in each aligned block of 256 rows (0 to 255, 256 to 511, ...) at most 4 rows name the same one
- bead_strip_destination: int32 [32768], P(('gx', 'gy')), may hold values from 0 to 127
Outputs:
- new_temperature: float32 [128, 128, 512], P('gx', 'gy', 'gz')
- residual: float32 [128, 128, 512], P('gx', 'gy', 'gz')
- deposited: float32 [128, 128, 512], P('gx', 'gy', 'gz')
The draws below stay inside these ranges and needn't reach their ends.
Inputs may be any that keep to these rules, and one draw needn't show every extreme that they name: `holding_tile_ordinal`: in the rows of one gx+gy position no owner is named by more than 4 rows, a bound that some block reaches.
All inputs are finite; a program needn't handle non-finite values.
Results may differ from the reference program's by a relative error of at most 0.0003.
Values sent between devices are 32-bit elements; how exact they have to be, the bound alone decides.
A program may use at most 64 MiB of HBM per device.

```python
import math
import jax
import jax.numpy as jnp
import numpy as np

CX = 8
CY = 16
REC = 256
CAP = 4
ITERS = 3
SEAM_LENGTH_NUM = 128
TRANSVERSE_COUNT = 128
PLATE_DEPTH_NUM = 512
ROWS = 32768
N_GX = 16
N_GY = 8


def plant(result, rng, low, largest):
    dims = result.shape
    place = [jax.random.randint(jax.random.fold_in(rng, axis), (), 0, dims[axis]) for axis in range(len(dims))]
    result = result.at[tuple(place)].set(low)
    longest = dims.index(max(dims))
    place[longest] = (place[longest] + 1) % dims[longest]
    return result.at[tuple(place)].set(largest)


def block_scale(own_key, extent, pieces, smallest, high):
    def one(axis_at, shards_of):
        heights = jax.random.uniform(jax.random.fold_in(jax.random.fold_in(own_key, 6), axis_at), (shards_of,), jnp.float32, smallest / len(pieces), high / len(pieces))
        return jnp.repeat(jnp.exp(heights), extent[axis_at] // shards_of).reshape((-1,) + (1,) * (len(extent) - axis_at - 1))

    level = one(*pieces[0])
    for cut in pieces[1:]:
        level = level * one(*cut)
    return level


def routed_block(own_key, own, number, rows, amount, top, most, skew):
    order = jax.random.permutation(own_key, amount)
    packed, common = portions_of(amount, rows * top, most, skew, True), portions_of(amount, rows * top, most, skew, False)
    places = jnp.arange(amount)

    def named(sizes, turn):
        used = int((sizes > 0).sum())
        fixed = max(1, used // 4)
        moved = fixed + (places - fixed + turn * (used - fixed)) % max(1, amount - fixed)
        return jnp.zeros((amount,), jnp.int32).at[order[jnp.where(places < fixed, places, moved)]].set(jnp.asarray(sizes, jnp.int32))

    sizes = jnp.where(number % 4 == 0, named(packed, number // 4), named(common, number - number // 4 - 1))
    mixed = jax.random.permutation(jax.random.fold_in(own, 3), amount)
    source_of, sink = mixed[0:amount // 2 * 2:2], mixed[1:amount // 2 * 2:2]
    margin = jnp.minimum(sizes[source_of] - 1, most - sizes[sink]) // 2
    margin = jnp.where((source_of == order[0]) | (sink == order[0]) | (sizes[sink] == 0), 0, jnp.maximum(margin, 0))
    moved = jax.random.randint(jax.random.fold_in(own, 4), (amount // 2,), 0, 1 << 20) % (margin + 1)
    sizes = sizes.at[source_of].add(-moved).at[sink].add(moved)
    items = jnp.searchsorted(jnp.cumsum(sizes), jnp.arange(rows * top), side="right").astype(jnp.int32)
    table = items.reshape(top, rows).T
    table = table[jax.random.permutation(jax.random.fold_in(own, 1), rows)]
    turn = jax.random.randint(jax.random.fold_in(own, 2), (rows, 1), 0, top)
    return jnp.take_along_axis(table, (jnp.arange(top)[None, :] + turn) % top, axis=1)


def portions_of(count, total, bound, slope, full):
    loads = [(1 << 20) // math.isqrt(grade ** slope) + 1 for grade in range(1, count + 1)]
    largest = bound if full else min(bound, max(-(-total // count), total * loads[0] // sum(loads)))
    least = 1 if total - largest >= count - 1 else 0
    given, rest = [largest] + [least] * (count - 1), total - largest - least * (count - 1)
    while rest > 0:
        free = [i for i in range(1, count) if given[i] < largest] or [i for i in range(1, count) if given[i] < bound]
        mass, remaining = sum([loads[i] for i in free]), rest
        for i in free:
            addition = min(bound - given[i], max(1, remaining * loads[i] // mass), rest)
            given[i] = given[i] + addition
            rest = rest - addition
    return np.array(given)


def centred(rng, dims, scale, most, cuts=(), held_as=jnp.bfloat16):
    factor_of = block_scale(rng, dims, cuts, -0.22, 0.18) if cuts else 1.0
    result = jax.random.normal(rng, dims, jnp.float32) * scale * factor_of
    return jnp.minimum(jnp.maximum(result, -most), most).astype(held_as)


def setup_inputs(seed: int = 0) -> dict:
    seeds = jax.random.split(jax.random.key(seed), 6)
    prior_thermal_state = centred(seeds[0], (SEAM_LENGTH_NUM, TRANSVERSE_COUNT, PLATE_DEPTH_NUM), 1.0, 6.0, ((0, 16), (1, 8), (2, 4)), jnp.float32)
    diffusivity_root_factor = jnp.clip(jnp.exp(math.log(1.5) - 1.0986123 * jax.random.uniform(seeds[1], (SEAM_LENGTH_NUM, TRANSVERSE_COUNT, PLATE_DEPTH_NUM), jnp.float32) ** block_scale(seeds[1], (SEAM_LENGTH_NUM, TRANSVERSE_COUNT, PLATE_DEPTH_NUM), ((0, 16), (1, 8), (2, 4)), -0.2, 0.2)), 0.5, 1.5)
    bead_strip_energy = centred(seeds[2], (ROWS, PLATE_DEPTH_NUM), 1.0, 6.0, ((0, 128), (1, 4)), jnp.float32)
    holding_tile_ordinal_keys = jax.random.split(jax.random.fold_in(seeds[3], 1), ROWS // REC)
    holding_tile_ordinal_turns = jax.random.permutation(jax.random.fold_in(seeds[3], 3), ROWS // REC)
    holding_tile_ordinal = jax.vmap(lambda own, number: routed_block(jax.random.fold_in(seeds[3], 2), own, number, REC, N_GX * N_GY, 1, CAP, 2))(holding_tile_ordinal_keys, holding_tile_ordinal_turns).reshape((ROWS, 1))
    bead_strip_destination = plant(jax.random.randint(seeds[4], (ROWS,), 0, CX * CY), jax.random.fold_in(seeds[4], 1), 0, (CX * CY) - 1).astype(jnp.int32)
    return {"prior_thermal_state": prior_thermal_state, "diffusivity_root_factor": diffusivity_root_factor, "bead_strip_energy": bead_strip_energy, "holding_tile_ordinal": holding_tile_ordinal, "bead_strip_destination": bead_strip_destination}


def neighbours(padded, array_extent):
    total = jnp.zeros(array_extent, jnp.float32)
    for dx in (-1, 0, 1):
        for dy in (-1, 0, 1):
            for dz in (-1, 0, 1):
                reach = abs(dx) + abs(dy) + abs(dz)
                if reach == 0:
                    continue
                weight = 0.5 ** (reach - 1)
                total = total + weight * padded[1 + dx:1 + dx + array_extent[0], 1 + dy:1 + dy + array_extent[1], 1 + dz:1 + dz + array_extent[2]]
    return total


def operate(field, diffusivity_root_factor):
    padded = jnp.pad(diffusivity_root_factor * field, 1)
    return (1.0 + 10.5 * diffusivity_root_factor) * field - 0.5 * diffusivity_root_factor * neighbours(padded, field.shape)


def reference(prior_thermal_state, diffusivity_root_factor, bead_strip_energy, holding_tile_ordinal, bead_strip_destination):
    owner = holding_tile_ordinal[:, 0]
    tile_seamwise_coord = (owner // N_GY) * CX + bead_strip_destination // CY
    tile_transverse_coord = (owner % N_GY) * CY + bead_strip_destination % CY
    energy_received = prior_thermal_state.at[tile_seamwise_coord, tile_transverse_coord, :].add(bead_strip_energy)
    diag = 1.0 + 10.5 * diffusivity_root_factor
    solution = energy_received
    resid = energy_received - operate(solution, diffusivity_root_factor)
    precond = resid / diag
    direction = precond
    rz_now = jnp.sum(resid * precond)
    for step in range(ITERS):
        image = operate(direction, diffusivity_root_factor)
        alpha = rz_now / jnp.sum(direction * image)
        solution = solution + alpha * direction
        resid = resid - alpha * image
        precond = resid / diag
        rz_next = jnp.sum(resid * precond)
        direction = precond + (rz_next / rz_now) * direction
        rz_now = rz_next
    return solution, resid, energy_received
```

```python
import functools

import jax
import jax.numpy as jnp
from jax import lax
from jax.experimental import pallas as pl
from jax.experimental.pallas import tpu as pltpu
from jax.sharding import PartitionSpec as P

MESH = pl.DeviceIdType.MESH
F32 = jnp.float32
BF16 = jnp.bfloat16
NX, NY, NZ = 16, 8, 4
CX, CY, CZ = 8, 16, 128
EX, EY = 16, 24
CAP = 4
AROUND = [(a, b, c) for a in (-1, 0, 1) for b in (-1, 0, 1) for c in (-1, 0, 1) if (a, b, c) != (0, 0, 0)]


def iota(shape, dim):
    return lax.broadcasted_iota(jnp.int32, shape, dim)


def dot_nn(a, b):
    return lax.dot_general(a, b, (((1,), (0,)), ((), ())), preferred_element_type=F32)


def dot_nt(a, b):
    return lax.dot_general(a, b, (((1,), (1,)), ((), ())), preferred_element_type=F32)


def three(v):
    hi = v.astype(BF16)
    rest = v - hi.astype(F32)
    mid = rest.astype(BF16)
    low = (rest - mid.astype(F32)).astype(BF16)
    return jnp.concatenate([hi, mid, low], axis=1)


def picked(onehot, parts):
    out = dot_nn(onehot, parts)
    n = out.shape[1] // 3
    return (out[:, 2 * n :] + out[:, n : 2 * n]) + out[:, :n]


def two_sum(a, b):
    s = a + b
    t = s - a
    return s, (a - (s - t)) + (b - t)


def quick_sum(a, b):
    s = a + b
    return s, b - (s - a)


def halves(a):
    c = a * 4097.0
    hi = c - (c - a)
    return hi, a - hi


def two_prod(a, b, sa=None, sb=None):
    p = a * b
    ah, al = halves(a) if sa is None else sa
    bh, bl = halves(b) if sb is None else sb
    return p, ((ah * bh - p) + ah * bl + al * bh) + al * bl


def dd_add(a, b):
    s, e = two_sum(a[0], b[0])
    return quick_sum(s, e + (a[1] + b[1]))


def dd_neg(a):
    return -a[0], -a[1]


def dd_sub(a, b):
    return dd_add(a, dd_neg(b))


def dd_mul(a, b):
    p, e = two_prod(a[0], b[0])
    return quick_sum(p, e + (a[0] * b[1] + a[1] * b[0]))


def dd_div(a, b):
    q = a[0] / b[0]
    r = dd_sub(a, dd_mul((q, jnp.zeros_like(q)), b))
    q2 = r[0] / b[0]
    r = dd_sub(r, dd_mul((q2, jnp.zeros_like(q)), b))
    return dd_add(quick_sum(q, q2), (r[0] / b[0], jnp.zeros_like(q)))


def tree(values, add):
    while len(values) > 1:
        values = [add(*values[i : i + 2]) if i + 1 < len(values) else values[i] for i in range(0, len(values), 2)]
    return values[0]


def coefficients(m):
    d = [dd_sub(m[k], m[k + 1]) for k in range(5)]
    one = (jnp.ones_like(m[0][0]), jnp.zeros_like(m[0][0]))
    a0 = dd_div(m[0], d[0])
    b = dd_sub(one, a0)
    rz1 = dd_mul(a0, dd_add(dd_mul(b, m[1]), dd_mul(a0, m[2])))
    p0 = dd_add(b, dd_div(rz1, m[0]))
    pq1 = dd_mul(a0, dd_add(dd_mul(p0, d[1]), dd_mul(a0, d[2])))
    a1 = dd_div(rz1, pq1)
    z0 = dd_sub(b, dd_mul(a1, p0))
    z1 = dd_sub(a0, dd_mul(a1, dd_sub(a0, p0)))
    z2 = dd_mul(a1, a0)
    rz2 = dd_mul(z2, dd_add(dd_add(dd_mul(z0, m[2]), dd_mul(z1, m[3])), dd_mul(z2, m[4])))
    be = dd_div(rz2, rz1)
    q0 = dd_add(z0, dd_mul(be, p0))
    q1 = dd_add(z1, dd_mul(be, a0))
    pq2 = dd_mul(z2, dd_add(dd_add(dd_mul(q0, d[2]), dd_mul(q1, d[3])), dd_mul(z2, d[4])))
    a2 = dd_div(rz2, pq2)
    xs = [
        dd_add(dd_add(a0, dd_mul(a1, p0)), dd_mul(a2, q0)),
        dd_add(dd_mul(a1, a0), dd_mul(a2, q1)),
        dd_mul(a2, z2),
    ]
    rs = [
        dd_sub(z0, dd_mul(a2, q0)),
        dd_sub(z1, dd_mul(a2, dd_sub(q1, q0))),
        dd_sub(z2, dd_mul(a2, dd_sub(z2, q1))),
        dd_mul(a2, z2),
    ]
    return [x[0] for x in xs], [r[0] for r in rs]


def faces(block):
    lane = iota((8, CZ), 1)
    group = ((lane + 4) // 8) % 16
    out = jnp.zeros((8, CZ), F32)
    for k in range(16):
        x, half = k // 2, k % 2
        tile = block[x, 8 * half : 8 * half + 8, :]
        out = jnp.where(group == k, pltpu.roll(tile, 8 * k, 1) if k else tile, out)
    return out


def spread_faces(plus, minus, out):
    lane = iota((8, CZ), 1)
    low = lane % 8 < 4
    upper = iota((8, CZ), 0) < 4
    keep = (lane < 4) | (lane >= 124)
    packs = {}
    for dx in (-1, 0, 1):
        for dy in (-1, 0, 1):
            i = (dx + 1) * 3 + dy + 1
            packs[dx, dy] = jnp.where(low, plus[i], minus[i])

    def moved(tile, k):
        return pltpu.roll(tile, CZ - 8 * k, 1) if k else tile

    for xp in range(EX):
        dx, x = (0, xp) if xp < 8 else ((1, xp - 8) if xp < 12 else (-1, xp - 8))
        for half in range(2):
            out[xp, 8 * half : 8 * half + 8, :] = jnp.where(keep, moved(packs[dx, 0], 2 * x + half), 0.0)
        both = jnp.where(upper, moved(packs[dx, 1], 2 * x), moved(packs[dx, -1], 2 * x + 1))
        out[xp, 16:24, :] = jnp.where(keep, both, 0.0)


def smooth_zy(m, a):
    lane = iota(m.shape, 1)
    first, last = lane == 0, lane == CZ - 1
    rm, ra = pltpu.roll(m, 1, 1), pltpu.roll(a, 1, 1)
    lm, la = pltpu.roll(m, CZ - 1, 1), pltpu.roll(a, CZ - 1, 1)
    m = m + 0.5 * (jnp.where(first, ra, rm) + jnp.where(last, la, lm))
    a = a + 0.5 * (jnp.where(first, rm, ra) + jnp.where(last, lm, la))

    def along_y(v):
        return v + 0.5 * (pltpu.roll(v, 1, 0) + pltpu.roll(v, EY - 1, 0))

    return along_y(m), along_y(a)


def kernel(
    owner_ref, dest_ref, prior_ref, h_ref, heat_ref,
    temp_out, resid_out, dep_out,
    heat, prior, hown, hm, ha, xm, ha_plus, ha_minus, xa, xa_plus, xa_minus,
    hy_plus, hy_minus, xy_plus, xy_minus, hpack, xpack, em, ea,
    send, held, rows, dsend, dheld, dtable, part_a, part_b, t_buf, r_buf,
    in_sem, out_sem, s1, r1, s2, r2, ds1, dr1, ds2, dr2, hs, hr, xs_, xr, as_, ar, bs, br,
):
    gx, gy, gz = lax.axis_index("gx"), lax.axis_index("gy"), lax.axis_index("gz")

    def at(a, b, c):
        return (lax.rem(gx + a + NX, NX), lax.rem(gy + b + NY, NY), lax.rem(gz + c + NZ, NZ))

    def remote(src, dst, ss, rs, to):
        return pltpu.make_async_remote_copy(
            src_ref=src, dst_ref=dst, send_sem=ss, recv_sem=rs, device_id=to, device_id_type=MESH
        )

    loads = [
        pltpu.make_async_copy(heat_ref, heat, in_sem.at[0]),
        pltpu.make_async_copy(h_ref, hown, in_sem.at[1]),
        pltpu.make_async_copy(prior_ref, prior, in_sem.at[2]),
    ]
    for c in loads:
        c.start()

    partners = set(AROUND)
    partners |= {(k, 0, 0) for k in range(1, NX)}
    partners |= {(0, j, l) for j in range(NY) for l in range(NZ)} - {(0, 0, 0)}
    partners = sorted({(a % NX, b % NY, c % NZ) for a, b, c in partners})
    barrier = pltpu.get_barrier_semaphore()
    for p in partners:
        pl.semaphore_signal(barrier, inc=1, device_id=at(*p), device_id_type=MESH)

    owner = owner_ref[...]
    dest = dest_ref[...]
    ox, oy = owner // NY, owner % NY
    kx = (ox - gx + NX) % NX
    jy = (oy - gy + NY) % NY
    rel = kx * NY + jy
    n_rows = owner.shape[1]
    named = rel == iota((NX * NY, n_rows), 0)
    earlier = (iota((n_rows, n_rows), 0) < iota((n_rows, n_rows), 1)).astype(F32).astype(BF16)
    rank = dot_nn(named.astype(F32).astype(BF16), earlier)
    rank_row = jnp.sum(jnp.where(named, rank, 0.0), axis=0, keepdims=True)
    slot = jy * CAP + rank_row.astype(jnp.int32)
    ahead = jnp.where(kx == iota((NX, n_rows), 0), (dest + 1).astype(F32), 0.0).astype(BF16)
    at_slot = (slot == iota((128, n_rows), 0)).astype(F32).astype(BF16)
    table = dot_nt(ahead, at_slot)
    dsend[...] = table.reshape(NX, 1, 128)
    dheld[0] = dsend[0]
    loads[0].wait()
    parts = three(heat[...])
    for c in range(CAP):
        mine = (named & (rank == float(c))).astype(F32).astype(BF16)
        packed = picked(mine, parts).reshape(NX, NY, CZ)
        send[:, :, c, :] = packed
        held[0, :, c, :] = packed[0]

    pl.semaphore_wait(barrier, len(partners))

    for k in range(1, NX):
        remote(dsend.at[k], dheld.at[k], ds1, dr1, at(k, 0, 0)).start()
    for k in range(1, NX):
        remote(send.at[k], held.at[k], s1, r1, at(k, 0, 0)).start()

    def exchange(own, wide, plus, minus, y_plus, y_minus, pack, ss, rs):
        for a, b in ((-1, 0), (1, 0), (0, -1), (0, 1), (-1, -1), (1, -1), (-1, 1), (1, 1)):
            xs = {-1: (0, 4), 0: (0, 8), 1: (4, 4)}[a]
            to = {-1: 8, 0: 0, 1: 12}[a]
            to_x = pl.ds(to, xs[1])
            from_x = pl.ds(*xs)
            if b == 0:
                remote(own.at[from_x], wide.at[to_x, pl.ds(0, CY)], ss.at[0], rs.at[0], at(a, b, 0)).start()
            elif b == -1:
                remote(own.at[from_x, pl.ds(0, 8)], y_plus.at[to_x], ss.at[1], rs.at[1], at(a, b, 0)).start()
            else:
                remote(own.at[from_x, pl.ds(8, 8)], y_minus.at[to_x], ss.at[2], rs.at[2], at(a, b, 0)).start()
        pack[...] = faces(own)
        for a in (-1, 0, 1):
            for b in (-1, 0, 1):
                i = (1 - a) * 3 + 1 - b
                remote(pack, plus.at[i], ss.at[3], rs.at[3], at(a, b, -1)).start()
                remote(pack, minus.at[i], ss.at[4], rs.at[4], at(a, b, 1)).start()

    def exchanged(wide, plus, minus, y_plus, y_minus, ss, rs):
        x_part = wide.at[pl.ds(8, 8), pl.ds(0, CY)]
        return [
            remote(v, v, ss.at[i], rs.at[i], at(1, 0, 0))
            for i, v in enumerate((x_part, y_plus, y_minus, plus, minus))
        ]

    loads[1].wait()
    exchange(hown, hm, ha_plus, ha_minus, hy_plus, hy_minus, hpack, hs, hr)
    hm[0:CX, 0:CY, :] = hown[...]

    d_along = remote(dsend.at[pl.ds(1, NX - 1)], dheld.at[pl.ds(1, NX - 1)], ds1, dr1, at(1, 0, 0))
    d_along.wait_recv()
    for j in range(1, NY):
        remote(dheld, dtable.at[j], ds2, dr2, at(0, j, 0)).start()

    h_waits = exchanged(hm, ha_plus, ha_minus, hy_plus, hy_minus, hs, hr)
    for w in h_waits:
        w.wait_recv()
    spread_faces(ha_plus, ha_minus, ha)
    upper = iota((EX, 8, CZ), 1) < 4
    hm[:, CY:EY, :] = jnp.where(upper, hy_plus[...], hy_minus[...])

    def inside(i, n):
        return (i < n - 1).astype(F32), (i > 0).astype(F32)

    (x_hi, x_lo), (y_hi, y_lo), (z_hi, z_lo) = inside(gx, NX), inside(gy, NY), inside(gz, NZ)
    row = iota((EY, CZ), 0)
    y_mask = jnp.where(row < CY, 1.0, jnp.where(row < CY + 4, y_hi, y_lo))
    z_mask = jnp.where(iota((EY, CZ), 1) < CZ // 2, z_hi, z_lo)
    for xp in range(EX):
        scale = y_mask if xp < CX else y_mask * (x_hi if xp < 12 else x_lo)
        h0 = hm[xp] * scale
        h1 = ha[xp] * (scale * z_mask)
        hm[xp] = h0
        ha[xp] = h1
        em[xp] = h0 * h0 / (1.0 + 10.5 * h0)
        ea[xp] = h1 * h1 / (1.0 + 10.5 * h1)

    along = remote(send.at[pl.ds(1, NX - 1)], held.at[pl.ds(1, NX - 1)], s1, r1, at(1, 0, 0))
    along.wait_recv()
    for j in range(1, NY):
        remote(held.at[:, j], rows.at[j], s2, r2, at(0, j, 0)).start()

    d_across = remote(dtable.at[pl.ds(1, NY - 1)], dtable.at[pl.ds(1, NY - 1)], ds2, dr2, at(0, 1, 0))
    d_across.wait_recv()
    dtable[0] = dheld[...]
    places = dtable[...].reshape(NY * NX, 128)
    own_lanes = iota((NY * NX, 128), 1) // CAP == iota((NY * NX, 128), 0) // NX
    places = jnp.where(own_lanes, places, 0.0).astype(BF16)
    cell = (iota((CX * CY, 128), 0) + 1).astype(F32)
    landing = []
    for c in range(CAP):
        lanes = (iota((CX * CY, 128), 1) % CAP == c).astype(F32).astype(BF16)
        landing.append((dot_nt(lanes, places) == cell).astype(F32).astype(BF16))
    landing = jnp.concatenate(landing, axis=1)

    across = remote(rows.at[pl.ds(1, NY - 1)], rows.at[pl.ds(1, NY - 1)], s2, r2, at(0, 1, 0))
    across.wait_recv()
    rows[0] = held[:, 0]
    arrived = jnp.concatenate([rows[:, :, c, :].reshape(NY * NX, CZ) for c in range(CAP)], axis=0)
    loads[2].wait()
    prior[...] = prior[...] + picked(landing, three(arrived)).reshape(CX, CY, CZ)
    dep_copy = pltpu.make_async_copy(prior, dep_out, out_sem.at[0])

    exchange(prior, xm, xa_plus, xa_minus, xy_plus, xy_minus, xpack, xs_, xr)
    dep_copy.start()
    xm[0:CX, 0:CY, :] = prior[...]
    x_waits = exchanged(xm, xa_plus, xa_minus, xy_plus, xy_minus, xs_, xr)
    for w in x_waits:
        w.wait_recv()
    spread_faces(xa_plus, xa_minus, xa)
    xm[:, CY:EY, :] = jnp.where(upper, xy_plus[...], xy_minus[...])

    def cells(width):
        return list(range(CX + width)) + list(range(EX - width, EX))

    def filtered(m, a, width):
        t = {x: smooth_zy(m[x], a[x]) for x in cells(width + 1)}
        out = {}
        for x in cells(width):
            lo, mid, hi = t[(x - 1) % EX], t[x], t[(x + 1) % EX]
            out[x] = tuple(mid[i] + 0.5 * (lo[i] + hi[i]) for i in range(2))
        return out

    m = {x: xm[x] * hm[x] for x in range(EX)}
    a = {x: xa[x] * ha[x] for x in range(EX)}
    us, gs = [], []
    for step in range(4):
        width = 3 - step
        t = filtered(m, a, width)
        um, ua = {}, {}
        for x in cells(width):
            um[x] = t[x][0] - m[x]
            ua[x] = t[x][1] - a[x]
            if step == 0:
                um[x] = um[x] - 10.5 * xm[x]
                ua[x] = ua[x] - 10.5 * xa[x]
        m = {x: em[x] * um[x] for x in cells(width)}
        a = {x: ea[x] * ua[x] for x in cells(width)}
        us.append([um[x][0:CY] for x in range(CX)])
        gs.append([m[x][0:CY] for x in range(CX)])

    us = [[halves(u) + (u,) for u in v] for v in us]
    gs_s = [[halves(g) + (g,) for g in v] for v in gs[:3]]
    row8 = iota((8, CZ), 0)
    lane8 = iota((8, CZ), 1)

    def pair_add(p, q):
        s, e = two_sum(p[0], q[0])
        return s, e + (p[1] + q[1])

    total = None
    for k, (i, j) in enumerate(((0, 0), (0, 1), (1, 1), (1, 2), (2, 2), (2, 3))):
        terms = []
        for x in range(CX):
            p, e = two_prod(gs_s[i][x][2], us[j][x][2], gs_s[i][x][:2], us[j][x][:2])
            terms += [(p[0:8], e[0:8]), (p[8:16], e[8:16])]
        v = tree(terms, pair_add)
        for shift in (4, 2, 1):
            v = pair_add(v, tuple(pltpu.roll(w, 8 - shift, 0) for w in v))
        v = pair_add(v, tuple(pltpu.roll(w, 64, 1) for w in v))
        v = jnp.where(lane8 < 64, v[0], v[1])
        total = v if total is None else jnp.where(row8 == k, v, total)
    part_a[0] = total

    def all_of(buf, n):
        s, e = tree([(buf[i], jnp.zeros((8, CZ), F32)) for i in range(n)], pair_add)
        return s + pltpu.roll(jnp.where(lane8 < 64, e, 0.0), 64, 1)

    for j in range(NY):
        for l in range(NZ):
            if j or l:
                remote(part_a.at[0], part_a.at[j * NZ + l], as_, ar, at(0, j, l)).start()
    a_all = remote(part_a.at[pl.ds(1, NY * NZ - 1)], part_a.at[pl.ds(1, NY * NZ - 1)], as_, ar, at(0, 1, 0))
    a_all.wait_recv()
    part_b[0] = all_of(part_a, NY * NZ)
    for k in range(1, NX):
        remote(part_b.at[0], part_b.at[k], bs, br, at(k, 0, 0)).start()
    b_all = remote(part_b.at[pl.ds(1, NX - 1)], part_b.at[pl.ds(1, NX - 1)], bs, br, at(1, 0, 0))
    b_all.wait_recv()
    s = all_of(part_b, NX)
    v = (s, pltpu.roll(s, 64, 1))
    for shift in (32, 16, 8, 4, 2, 1):
        v = pair_add(v, tuple(pltpu.roll(w, CZ - shift, 1) for w in v))
    v = quick_sum(*v)
    moments = [(v[0][k : k + 1, 0:1], v[1][k : k + 1, 0:1]) for k in range(6)]

    xs, rs = coefficients(moments)
    xs = [jnp.broadcast_to(c, (CY, CZ)) for c in xs]
    rs = [jnp.broadcast_to(c, (CY, CZ)) for c in rs]
    for x in range(CX):
        h = hown[x]
        over = 1.0 / h
        t_buf[x] = prior[x] + (xs[0] * gs[0][x] + xs[1] * gs[1][x] + xs[2] * gs[2][x]) * over
        mix = (rs[0] * gs[0][x] + rs[1] * gs[1][x]) + (rs[2] * gs[2][x] + rs[3] * gs[3][x])
        r_buf[x] = mix * (over + 10.5)
    outs = [
        pltpu.make_async_copy(t_buf, temp_out, out_sem.at[1]),
        pltpu.make_async_copy(r_buf, resid_out, out_sem.at[2]),
    ]
    for c in outs:
        c.start()
    for w in [d_along, along, d_across, across] + h_waits + x_waits + [a_all, b_all]:
        if w is d_across:
            for j in range(1, NY):
                remote(dheld, dtable.at[j], ds2, dr2, at(0, j, 0)).wait_send()
        else:
            w.wait_send()
    dep_copy.wait()
    for c in outs:
        c.wait()


def local(prior, h, heat, owner, dest):
    n = dest.shape[0]
    any_ = pl.BlockSpec(memory_space=pl.ANY)
    vmem = pl.BlockSpec(memory_space=pltpu.VMEM)
    block = jax.ShapeDtypeStruct((CX, CY, CZ), F32)
    V = lambda *shape: pltpu.VMEM(shape, F32)
    D = pltpu.SemaphoreType.DMA
    wide = V(EX, EY, CZ)
    nine, ys, tile = V(9, 8, CZ), V(EX, 8, CZ), V(8, CZ)
    own = V(CX, CY, CZ)
    scratch = [
        V(n, CZ), own, own, wide, wide, wide, nine, nine, wide, nine, nine,
        ys, ys, ys, ys, tile, tile, wide, wide,
        V(NX, NY, CAP, CZ), V(NX, NY, CAP, CZ), V(NY, NX, CAP, CZ),
        V(NX, 1, 128), V(NX, 1, 128), V(NY, NX, 1, 128),
        V(NY * NZ, 8, CZ), V(NX, 8, CZ), own, own,
        D((3,)), D((3,)), D, D, D, D, D, D, D, D,
        D((5,)), D((5,)), D((5,)), D((5,)), D, D, D, D,
    ]
    return pl.pallas_call(
        kernel,
        out_shape=(block, block, block),
        in_specs=[vmem, vmem, any_, any_, any_],
        out_specs=(any_, any_, any_),
        scratch_shapes=scratch,
        compiler_params=pltpu.CompilerParams(
            collective_id=0, has_side_effects=True, vmem_limit_bytes=48 * 1024 * 1024
        ),
    )(owner.reshape(1, n), dest.reshape(1, n), prior, h, heat)


def solution(mesh):
    placed = (
        P("gx", "gy", "gz"),
        P("gx", "gy", "gz"),
        P(("gx", "gy"), "gz"),
        P(("gx", "gy"), None),
        P(("gx", "gy")),
    )
    return jax.shard_map(
        local,
        mesh=mesh,
        in_specs=placed,
        out_specs=(P("gx", "gy", "gz"), P("gx", "gy", "gz"), P("gx", "gy", "gz")),
        check_vma=False,
    )
```

```python
import jax
import jax.numpy as jnp
from jax import lax
from jax.experimental import pallas as pl
from jax.experimental.pallas import tpu as pltpu
from jax.sharding import PartitionSpec as P

MESH = pl.DeviceIdType.MESH
F32 = jnp.float32
BF16 = jnp.bfloat16
NX, NY, NZ = 16, 8, 4
CX, CY, CZ = 8, 16, 128
EX, EY = 16, 24
CAP = 4
VMEM_BYTES = 60 * 1024 * 1024
NEAR = 9
FAR_FIRST = [8, 7, 9, 6, 10, 5, 11, 4, 12, 3, 13, 2, 14, 1, 15]
AROUND = [(a, b, c) for a in (-1, 0, 1) for b in (-1, 0, 1) for c in (-1, 0, 1) if (a, b, c) != (0, 0, 0)]


def iota(shape, dim):
    return lax.broadcasted_iota(jnp.int32, shape, dim)


def dot_nn(a, b):
    return lax.dot_general(a, b, (((1,), (0,)), ((), ())), preferred_element_type=F32)


def dot_nt(a, b):
    return lax.dot_general(a, b, (((1,), (1,)), ((), ())), preferred_element_type=F32)


def three(v):
    hi = v.astype(BF16)
    rest = v - hi.astype(F32)
    mid = rest.astype(BF16)
    low = (rest - mid.astype(F32)).astype(BF16)
    return jnp.concatenate([hi, mid, low], axis=1)


def picked(onehot, parts):
    out = dot_nn(onehot, parts)
    n = out.shape[1] // 3
    return (out[:, 2 * n :] + out[:, n : 2 * n]) + out[:, :n]


def two_sum(a, b):
    s = a + b
    t = s - a
    return s, (a - (s - t)) + (b - t)


def quick_sum(a, b):
    s = a + b
    return s, b - (s - a)


def halves(a):
    c = a * 4097.0
    hi = c - (c - a)
    return hi, a - hi


def two_prod(a, b, sa=None, sb=None):
    p = a * b
    ah, al = halves(a) if sa is None else sa
    bh, bl = halves(b) if sb is None else sb
    return p, ((ah * bh - p) + ah * bl + al * bh) + al * bl


def dd_add(a, b):
    s, e = two_sum(a[0], b[0])
    return quick_sum(s, e + (a[1] + b[1]))


def dd_neg(a):
    return -a[0], -a[1]


def dd_sub(a, b):
    return dd_add(a, dd_neg(b))


def dd_mul(a, b):
    p, e = two_prod(a[0], b[0])
    return quick_sum(p, e + (a[0] * b[1] + a[1] * b[0]))


def dd_div(a, b):
    q = a[0] / b[0]
    r = dd_sub(a, dd_mul((q, jnp.zeros_like(q)), b))
    q2 = r[0] / b[0]
    r = dd_sub(r, dd_mul((q2, jnp.zeros_like(q)), b))
    return dd_add(quick_sum(q, q2), (r[0] / b[0], jnp.zeros_like(q)))


def tree(values, add):
    while len(values) > 1:
        values = [add(*values[i : i + 2]) if i + 1 < len(values) else values[i] for i in range(0, len(values), 2)]
    return values[0]


def coefficients(m):
    d = [dd_sub(m[k], m[k + 1]) for k in range(5)]
    one = (jnp.ones_like(m[0][0]), jnp.zeros_like(m[0][0]))
    a0 = dd_div(m[0], d[0])
    b = dd_sub(one, a0)
    rz1 = dd_mul(a0, dd_add(dd_mul(b, m[1]), dd_mul(a0, m[2])))
    p0 = dd_add(b, dd_div(rz1, m[0]))
    pq1 = dd_mul(a0, dd_add(dd_mul(p0, d[1]), dd_mul(a0, d[2])))
    a1 = dd_div(rz1, pq1)
    z0 = dd_sub(b, dd_mul(a1, p0))
    z1 = dd_sub(a0, dd_mul(a1, dd_sub(a0, p0)))
    z2 = dd_mul(a1, a0)
    rz2 = dd_mul(z2, dd_add(dd_add(dd_mul(z0, m[2]), dd_mul(z1, m[3])), dd_mul(z2, m[4])))
    be = dd_div(rz2, rz1)
    q0 = dd_add(z0, dd_mul(be, p0))
    q1 = dd_add(z1, dd_mul(be, a0))
    pq2 = dd_mul(z2, dd_add(dd_add(dd_mul(q0, d[2]), dd_mul(q1, d[3])), dd_mul(z2, d[4])))
    a2 = dd_div(rz2, pq2)
    xs = [
        dd_add(dd_add(a0, dd_mul(a1, p0)), dd_mul(a2, q0)),
        dd_add(dd_mul(a1, a0), dd_mul(a2, q1)),
        dd_mul(a2, z2),
    ]
    rs = [
        dd_sub(z0, dd_mul(a2, q0)),
        dd_sub(z1, dd_mul(a2, dd_sub(q1, q0))),
        dd_sub(z2, dd_mul(a2, dd_sub(z2, q1))),
        dd_mul(a2, z2),
    ]
    return [x[0] for x in xs], [r[0] for r in rs]


def faces(block):
    lane = iota((8, CZ), 1)
    group = ((lane + 4) // 8) % 16
    out = jnp.zeros((8, CZ), F32)
    for k in range(16):
        x, half = k // 2, k % 2
        tile = block[x, 8 * half : 8 * half + 8, :]
        out = jnp.where(group == k, pltpu.roll(tile, 8 * k, 1) if k else tile, out)
    return out


def spread_faces(plus, minus, out):
    lane = iota((8, CZ), 1)
    low = lane % 8 < 4
    upper = iota((8, CZ), 0) < 4
    keep = (lane < 4) | (lane >= 124)
    packs = {}
    for dx in (-1, 0, 1):
        for dy in (-1, 0, 1):
            i = (dx + 1) * 3 + dy + 1
            packs[dx, dy] = jnp.where(low, plus[i], minus[i])

    def moved(tile, k):
        return pltpu.roll(tile, CZ - 8 * k, 1) if k else tile

    for xp in range(EX):
        dx, x = (0, xp) if xp < 8 else ((1, xp - 8) if xp < 12 else (-1, xp - 8))
        for half in range(2):
            out[xp, 8 * half : 8 * half + 8, :] = jnp.where(keep, moved(packs[dx, 0], 2 * x + half), 0.0)
        both = jnp.where(upper, moved(packs[dx, 1], 2 * x), moved(packs[dx, -1], 2 * x + 1))
        out[xp, 16:24, :] = jnp.where(keep, both, 0.0)


def smooth_zy(m, a):
    lane = iota(m.shape, 1)
    first, last = lane == 0, lane == CZ - 1
    rm, ra = pltpu.roll(m, 1, 1), pltpu.roll(a, 1, 1)
    lm, la = pltpu.roll(m, CZ - 1, 1), pltpu.roll(a, CZ - 1, 1)
    m = m + 0.5 * (jnp.where(first, ra, rm) + jnp.where(last, la, lm))
    a = a + 0.5 * (jnp.where(first, rm, ra) + jnp.where(last, lm, la))

    def along_y(v):
        return v + 0.5 * (pltpu.roll(v, 1, 0) + pltpu.roll(v, EY - 1, 0))

    return along_y(m), along_y(a)


def kernel(
    owner_ref, dest_ref, prior_ref, h_ref, heat_ref,
    temp_out, resid_out, dep_out,
    prior, owner_v, dest_v, heat, hown, hm, ha, xm, ha_plus, ha_minus, xa, xa_plus, xa_minus,
    hy_plus, hy_minus, xy_plus, xy_minus, hpack, xpack, em, ea,
    send, held, rows, dsend, dheld, dtable, part_a, part_b, t_buf, r_buf,
    in_sem, out_sem, s1, r1, s2, r2, ds1, dr1, ds2, dr2, hs, hr, xs_, xr, as_, ar, bs, br,
):
    gx, gy, gz = lax.axis_index("gx"), lax.axis_index("gy"), lax.axis_index("gz")

    def at(a, b, c):
        return (lax.rem(gx + a + NX, NX), lax.rem(gy + b + NY, NY), lax.rem(gz + c + NZ, NZ))

    def remote(src, dst, ss, rs, to):
        return pltpu.make_async_remote_copy(
            src_ref=src, dst_ref=dst, send_sem=ss, recv_sem=rs, device_id=to, device_id_type=MESH
        )

    loads = [
        pltpu.make_async_copy(heat_ref, heat, in_sem.at[0]),
        pltpu.make_async_copy(h_ref, hown, in_sem.at[1]),
        pltpu.make_async_copy(prior_ref, prior, in_sem.at[2]),
        pltpu.make_async_copy(owner_ref, owner_v, in_sem.at[3]),
        pltpu.make_async_copy(dest_ref, dest_v, in_sem.at[4]),
    ]
    for c in (loads[3], loads[4], loads[0], loads[1], loads[2]):
        c.start()

    partners = [(k, 0, 0) for k in FAR_FIRST] + [(0, j, 0) for j in (4, 3, 5, 2, 6, 1, 7)] + [(0, 0, l) for l in (2, 1, 3)]
    barrier = pltpu.get_barrier_semaphore()
    for p in partners:
        pl.semaphore_signal(barrier, inc=1, device_id=at(*p), device_id_type=MESH)

    loads[3].wait()
    loads[4].wait()
    owner = owner_v[...]
    dest = dest_v[...]
    ox, oy = owner // NY, owner % NY
    kx = (ox - gx + NX) % NX
    kx = jnp.where(kx == 0, 0, jnp.where(kx <= NX // 2, 2 * kx - 1, 2 * NX - 2 * kx))
    jy = (oy - gy + NY) % NY
    rel = kx * NY + jy
    n_rows = owner.shape[1]
    named = rel == iota((NX * NY, n_rows), 0)
    earlier = (iota((n_rows, n_rows), 0) < iota((n_rows, n_rows), 1)).astype(F32).astype(BF16)
    rank = dot_nn(named.astype(F32).astype(BF16), earlier)
    rank_row = jnp.sum(jnp.where(named, rank, 0.0), axis=0, keepdims=True)
    slot = jy * CAP + rank_row.astype(jnp.int32)
    ahead = jnp.where(kx == iota((NX, n_rows), 0), (dest + 1).astype(F32), 0.0).astype(BF16)
    at_slot = (slot == iota((128, n_rows), 0)).astype(F32).astype(BF16)
    table = dot_nt(ahead, at_slot)
    dsend[...] = table.reshape(NX, 1, 128)
    dheld[0] = dsend[0]
    loads[0].wait()
    parts = three(heat[...])
    for c in range(CAP):
        mine = (named & (rank == float(c))).astype(F32).astype(BF16)
        packed = picked(mine, parts).reshape(NX, NY, CZ)
        send[:, :, c, :] = packed
        held[0, :, c, :] = packed[0]

    pl.semaphore_wait(barrier, len(partners))

    def place(k):
        return 2 * k - 1 if k <= NX // 2 else 2 * NX - 2 * k

    for k in FAR_FIRST:
        remote(dsend.at[place(k)], dheld.at[place(k)], ds1, dr1, at(k, 0, 0)).start()
    for k in FAR_FIRST:
        i = int(place(k) >= NEAR)
        remote(send.at[place(k)], held.at[place(k)], s1.at[i], r1.at[i], at(k, 0, 0)).start()

    def exchange(own, wide, plus, minus, y_plus, y_minus, pack, ss, rs):
        for a, b in ((-1, 0), (1, 0), (0, -1), (0, 1), (-1, -1), (1, -1), (-1, 1), (1, 1)):
            xs = {-1: (0, 4), 0: (0, 8), 1: (4, 4)}[a]
            to = {-1: 8, 0: 0, 1: 12}[a]
            to_x = pl.ds(to, xs[1])
            from_x = pl.ds(*xs)
            if b == 0:
                remote(own.at[from_x], wide.at[to_x, pl.ds(0, CY)], ss.at[0], rs.at[0], at(a, b, 0)).start()
            elif b == -1:
                remote(own.at[from_x, pl.ds(0, 8)], y_plus.at[to_x], ss.at[1], rs.at[1], at(a, b, 0)).start()
            else:
                remote(own.at[from_x, pl.ds(8, 8)], y_minus.at[to_x], ss.at[2], rs.at[2], at(a, b, 0)).start()
        pack[...] = faces(own)
        for a in (-1, 0, 1):
            for b in (-1, 0, 1):
                i = (1 - a) * 3 + 1 - b
                remote(pack, plus.at[i], ss.at[3], rs.at[3], at(a, b, -1)).start()
                remote(pack, minus.at[i], ss.at[4], rs.at[4], at(a, b, 1)).start()

    def exchanged(wide, plus, minus, y_plus, y_minus, ss, rs):
        x_part = wide.at[pl.ds(8, 8), pl.ds(0, CY)]
        return [
            remote(v, v, ss.at[i], rs.at[i], at(1, 0, 0))
            for i, v in enumerate((x_part, y_plus, y_minus, plus, minus))
        ]

    d_along = remote(dsend.at[pl.ds(1, NX - 1)], dheld.at[pl.ds(1, NX - 1)], ds1, dr1, at(1, 0, 0))
    d_along.wait_recv()
    for j in range(1, NY):
        remote(dheld, dtable.at[j], ds2, dr2, at(0, j, 0)).start()

    chunks = ((1, NEAR), (NEAR, NX))
    along = []
    for i, (lo, hi) in enumerate(chunks):
        part = pl.ds(lo, hi - lo)
        along.append(remote(send.at[part], held.at[part], s1.at[i], r1.at[i], at(1, 0, 0)))
        along[i].wait_recv()
        part = pl.ds(lo if i else 0, hi - (lo if i else 0))
        for j in range(1, NY):
            remote(held.at[part, j], rows.at[j, part], s2.at[i], r2.at[i], at(0, j, 0)).start()

    d_across = remote(dtable.at[pl.ds(1, NY - 1)], dtable.at[pl.ds(1, NY - 1)], ds2, dr2, at(0, 1, 0))
    d_across.wait_recv()
    dtable[0] = dheld[...]

    loads[1].wait()
    exchange(hown, hm, ha_plus, ha_minus, hy_plus, hy_minus, hpack, hs, hr)
    hm[0:CX, 0:CY, :] = hown[...]

    places = dtable[...].reshape(NY * NX, 128)
    own_lanes = iota((NY * NX, 128), 1) // CAP == iota((NY * NX, 128), 0) // NX
    places = jnp.where(own_lanes, places, 0.0).astype(BF16)
    cell = (iota((CX * CY, 128), 0) + 1).astype(F32)
    landing = []
    for c in range(CAP):
        lanes = (iota((CX * CY, 128), 1) % CAP == c).astype(F32).astype(BF16)
        landing.append((dot_nt(lanes, places) == cell).astype(F32).astype(BF16))
    landing = jnp.concatenate(landing, axis=1)

    across = []
    for i, (lo, hi) in enumerate(chunks):
        part = pl.ds(lo if i else 0, hi - (lo if i else 0))
        across.append(remote(rows.at[pl.ds(1, NY - 1), part], rows.at[pl.ds(1, NY - 1), part], s2.at[i], r2.at[i], at(0, 1, 0)))
        across[i].wait_recv()
    rows[0] = held[:, 0]
    arrived = jnp.concatenate([rows[:, :, c, :].reshape(NY * NX, CZ) for c in range(CAP)], axis=0)
    loads[2].wait()
    prior[...] = prior[...] + picked(landing, three(arrived)).reshape(CX, CY, CZ)

    exchange(prior, xm, xa_plus, xa_minus, xy_plus, xy_minus, xpack, xs_, xr)
    dep_copy = pltpu.make_async_copy(prior, dep_out, out_sem.at[0])
    dep_copy.start()
    xm[0:CX, 0:CY, :] = prior[...]

    h_waits = exchanged(hm, ha_plus, ha_minus, hy_plus, hy_minus, hs, hr)
    for w in h_waits:
        w.wait_recv()
    spread_faces(ha_plus, ha_minus, ha)
    upper = iota((EX, 8, CZ), 1) < 4
    hm[:, CY:EY, :] = jnp.where(upper, hy_plus[...], hy_minus[...])

    def inside(i, n):
        return (i < n - 1).astype(F32), (i > 0).astype(F32)

    (x_hi, x_lo), (y_hi, y_lo), (z_hi, z_lo) = inside(gx, NX), inside(gy, NY), inside(gz, NZ)
    row = iota((EY, CZ), 0)
    y_mask = jnp.where(row < CY, 1.0, jnp.where(row < CY + 4, y_hi, y_lo))
    z_mask = jnp.where(iota((EY, CZ), 1) < CZ // 2, z_hi, z_lo)
    for xp in range(EX):
        scale = y_mask if xp < CX else y_mask * (x_hi if xp < 12 else x_lo)
        h0 = hm[xp] * scale
        h1 = ha[xp] * (scale * z_mask)
        hm[xp] = h0
        ha[xp] = h1
        em[xp] = h0 * h0 / (1.0 + 10.5 * h0)
        ea[xp] = h1 * h1 / (1.0 + 10.5 * h1)

    x_waits = exchanged(xm, xa_plus, xa_minus, xy_plus, xy_minus, xs_, xr)
    for w in x_waits:
        w.wait_recv()
    spread_faces(xa_plus, xa_minus, xa)
    xm[:, CY:EY, :] = jnp.where(upper, xy_plus[...], xy_minus[...])

    def cells(width):
        return list(range(CX + width)) + list(range(EX - width, EX))

    def filtered(m, a, width):
        t = {x: smooth_zy(m[x], a[x]) for x in cells(width + 1)}
        out = {}
        for x in cells(width):
            lo, mid, hi = t[(x - 1) % EX], t[x], t[(x + 1) % EX]
            out[x] = tuple(mid[i] + 0.5 * (lo[i] + hi[i]) for i in range(2))
        return out

    m = {x: xm[x] * hm[x] for x in range(EX)}
    a = {x: xa[x] * ha[x] for x in range(EX)}
    us, gs = [], []
    for step in range(4):
        width = 3 - step
        t = filtered(m, a, width)
        um, ua = {}, {}
        for x in cells(width):
            um[x] = t[x][0] - m[x]
            ua[x] = t[x][1] - a[x]
            if step == 0:
                um[x] = um[x] - 10.5 * xm[x]
                ua[x] = ua[x] - 10.5 * xa[x]
        m = {x: em[x] * um[x] for x in cells(width)}
        a = {x: ea[x] * ua[x] for x in cells(width)}
        us.append([um[x][0:CY] for x in range(CX)])
        gs.append([m[x][0:CY] for x in range(CX)])

    us = [[halves(u) + (u,) for u in v] for v in us]
    gs_s = [[halves(g) + (g,) for g in v] for v in gs[:3]]
    row8 = iota((8, CZ), 0)
    lane8 = iota((8, CZ), 1)

    def pair_add(p, q):
        s, e = two_sum(p[0], q[0])
        return s, e + (p[1] + q[1])

    high, rest = jnp.zeros((8, CZ), F32), jnp.zeros((8, CZ), F32)
    for k, (i, j) in enumerate(((0, 0), (0, 1), (1, 1), (1, 2), (2, 2), (2, 3))):
        terms = []
        for x in range(CX):
            p, e = two_prod(gs_s[i][x][2], us[j][x][2], gs_s[i][x][:2], us[j][x][:2])
            terms += [(p[0:8], e[0:8]), (p[8:16], e[8:16])]
        v = tree(terms, pair_add)
        for shift in (4, 2, 1):
            v = pair_add(v, tuple(pltpu.roll(w, shift, 0) for w in v))
        high, rest = jnp.where(row8 == k, v[0], high), jnp.where(row8 == k, v[1], rest)
    v = high, rest
    for shift in (64, 32, 16, 8, 4, 2, 1):
        v = pair_add(v, tuple(pltpu.roll(w, shift, 1) for w in v))
    v = jnp.where(lane8 == row8, v[0], jnp.where(lane8 == row8 + 64, v[1], 0.0))
    part_a[0] = jnp.sum(v, axis=0, keepdims=True)

    def all_of(buf, n):
        v = buf[...].reshape(n, CZ)
        v = tree([(v[8 * i : 8 * i + 8], jnp.zeros((8, CZ), F32)) for i in range(n // 8)], pair_add)
        for shift in (4, 2, 1):
            v = pair_add(v, tuple(pltpu.roll(w, shift, 0) for w in v))
        v = v[0] + pltpu.roll(jnp.where(lane8 < 64, v[1], 0.0), 64, 1)
        return v[0:1]

    for l in (2, 1, 3, 0):
        for j in (4, 3, 5, 2, 6, 1, 7, 0):
            if j or l:
                remote(part_a.at[0], part_a.at[j * NZ + l], as_, ar, at(0, j, l)).start()
    a_all = remote(part_a.at[pl.ds(1, NY * NZ - 1)], part_a.at[pl.ds(1, NY * NZ - 1)], as_, ar, at(0, 1, 0))
    a_all.wait_recv()
    part_b[0] = all_of(part_a, NY * NZ)
    for k in FAR_FIRST:
        remote(part_b.at[0], part_b.at[k], bs, br, at(k, 0, 0)).start()
    b_all = remote(part_b.at[pl.ds(1, NX - 1)], part_b.at[pl.ds(1, NX - 1)], bs, br, at(1, 0, 0))
    b_all.wait_recv()
    s = all_of(part_b, NX)
    moments = [quick_sum(s[:, k : k + 1], s[:, 64 + k : 65 + k]) for k in range(6)]

    xs, rs = coefficients(moments)
    xs = [jnp.broadcast_to(c, (CY, CZ)) for c in xs]
    rs = [jnp.broadcast_to(c, (CY, CZ)) for c in rs]
    for x in range(CX):
        h = hown[x]
        over = 1.0 / h
        t_buf[x] = prior[x] + (xs[0] * gs[0][x] + xs[1] * gs[1][x] + xs[2] * gs[2][x]) * over
        mix = (rs[0] * gs[0][x] + rs[1] * gs[1][x]) + (rs[2] * gs[2][x] + rs[3] * gs[3][x])
        r_buf[x] = mix * (over + 10.5)
    outs = [
        pltpu.make_async_copy(t_buf, temp_out, out_sem.at[1]),
        pltpu.make_async_copy(r_buf, resid_out, out_sem.at[2]),
    ]
    for c in outs:
        c.start()
    for w in [d_along] + along + across + h_waits + x_waits + [a_all, b_all]:
        w.wait_send()
    for j in range(1, NY):
        remote(dheld, dtable.at[j], ds2, dr2, at(0, j, 0)).wait_send()
    dep_copy.wait()
    for c in outs:
        c.wait()


def write_out(*refs):
    sems = refs[-1]
    n = len(refs) // 2
    copies = [pltpu.make_async_copy(refs[i], refs[n + i], sems.at[i]) for i in range(n)]
    for c in copies:
        c.start()
    for c in copies:
        c.wait()


def local(prior, h, heat, owner, dest):
    n = dest.shape[0]
    hbm = pl.BlockSpec(memory_space=pltpu.HBM)
    block = jax.ShapeDtypeStruct((CX, CY, CZ), F32)
    V = lambda *shape: pltpu.VMEM(shape, F32)
    D = pltpu.SemaphoreType.DMA
    wide = V(EX, EY, CZ)
    nine, ys, tile = V(9, 8, CZ), V(EX, 8, CZ), V(8, CZ)
    own = V(CX, CY, CZ)
    scratch = [
        own, pltpu.VMEM((1, n), jnp.int32), pltpu.VMEM((1, n), jnp.int32), V(n, CZ), own, wide, wide, wide, nine, nine, wide, nine, nine,
        ys, ys, ys, ys, tile, tile, wide, wide,
        V(NX, NY, CAP, CZ), V(NX, NY, CAP, CZ), V(NY, NX, CAP, CZ),
        V(NX, 1, 128), V(NX, 1, 128), V(NY, NX, 1, 128),
        V(NY * NZ, 1, CZ), V(NX, 1, CZ), own, own,
        D((5,)), D((3,)), D((2,)), D((2,)), D((2,)), D((2,)), D, D, D, D,
        D((5,)), D((5,)), D((5,)), D((5,)), D, D, D, D,
    ]
    outs = pl.pallas_call(
        kernel,
        out_shape=(block, block, block),
        in_specs=[hbm] * 5,
        out_specs=(hbm,) * 3,
        scratch_shapes=scratch,
        compiler_params=pltpu.CompilerParams(
            collective_id=0, has_side_effects=True, vmem_limit_bytes=VMEM_BYTES
        ),
    )(owner.reshape(1, n), dest.reshape(1, n), prior, h, heat)
    return pl.pallas_call(
        write_out,
        out_shape=(block, block, block),
        in_specs=[hbm] * 3,
        out_specs=(hbm,) * 3,
        scratch_shapes=[D((3,))],
        compiler_params=pltpu.CompilerParams(vmem_limit_bytes=VMEM_BYTES),
    )(*outs)


def solution(mesh):
    placed = (
        P("gx", "gy", "gz"),
        P("gx", "gy", "gz"),
        P(("gx", "gy"), "gz"),
        P(("gx", "gy"), None),
        P(("gx", "gy")),
    )
    return jax.shard_map(
        local,
        mesh=mesh,
        in_specs=placed,
        out_specs=(P("gx", "gy", "gz"), P("gx", "gy", "gz"), P("gx", "gy", "gz")),
        check_vma=False,
    )
```

```python
import jax
import jax.numpy as jnp
from jax import lax
from jax.experimental import pallas as pl
from jax.experimental.pallas import tpu as pltpu
from jax.sharding import PartitionSpec as P

MESH = pl.DeviceIdType.MESH
F32 = jnp.float32
BF16 = jnp.bfloat16
NX, NY, NZ = 16, 8, 4
CX, CY, CZ = 8, 16, 128
EX, EY = 16, 24
CAP = 4
VMEM_BYTES = 60 * 1024 * 1024
FAR_FIRST = [8, 7, 9, 6, 10, 5, 11, 4, 12, 3, 13, 2, 14, 1, 15]
AROUND = [(a, b, c) for a in (-1, 0, 1) for b in (-1, 0, 1) for c in (-1, 0, 1) if (a, b, c) != (0, 0, 0)]


def iota(shape, dim):
    return lax.broadcasted_iota(jnp.int32, shape, dim)


def dot_nn(a, b):
    return lax.dot_general(a, b, (((1,), (0,)), ((), ())), preferred_element_type=F32)


def dot_nt(a, b):
    return lax.dot_general(a, b, (((1,), (1,)), ((), ())), preferred_element_type=F32)


def three(v):
    hi = v.astype(BF16)
    rest = v - hi.astype(F32)
    mid = rest.astype(BF16)
    low = (rest - mid.astype(F32)).astype(BF16)
    return jnp.concatenate([hi, mid, low], axis=1)


def picked(onehot, parts):
    out = dot_nn(onehot, parts)
    n = out.shape[1] // 3
    return (out[:, 2 * n :] + out[:, n : 2 * n]) + out[:, :n]


def two_sum(a, b):
    s = a + b
    t = s - a
    return s, (a - (s - t)) + (b - t)


def quick_sum(a, b):
    s = a + b
    return s, b - (s - a)


def halves(a):
    c = a * 4097.0
    hi = c - (c - a)
    return hi, a - hi


def two_prod(a, b, sa=None, sb=None):
    p = a * b
    ah, al = halves(a) if sa is None else sa
    bh, bl = halves(b) if sb is None else sb
    return p, ((ah * bh - p) + ah * bl + al * bh) + al * bl


def dd_add(a, b):
    s, e = two_sum(a[0], b[0])
    return quick_sum(s, e + (a[1] + b[1]))


def dd_neg(a):
    return -a[0], -a[1]


def dd_sub(a, b):
    return dd_add(a, dd_neg(b))


def dd_mul(a, b):
    p, e = two_prod(a[0], b[0])
    return quick_sum(p, e + (a[0] * b[1] + a[1] * b[0]))


def dd_div(a, b):
    q = a[0] / b[0]
    r = dd_sub(a, dd_mul((q, jnp.zeros_like(q)), b))
    q2 = r[0] / b[0]
    r = dd_sub(r, dd_mul((q2, jnp.zeros_like(q)), b))
    return dd_add(quick_sum(q, q2), (r[0] / b[0], jnp.zeros_like(q)))


def tree(values, add):
    while len(values) > 1:
        values = [add(*values[i : i + 2]) if i + 1 < len(values) else values[i] for i in range(0, len(values), 2)]
    return values[0]


def coefficients(m):
    d = [dd_sub(m[k], m[k + 1]) for k in range(5)]
    one = (jnp.ones_like(m[0][0]), jnp.zeros_like(m[0][0]))
    a0 = dd_div(m[0], d[0])
    b = dd_sub(one, a0)
    rz1 = dd_mul(a0, dd_add(dd_mul(b, m[1]), dd_mul(a0, m[2])))
    p0 = dd_add(b, dd_div(rz1, m[0]))
    pq1 = dd_mul(a0, dd_add(dd_mul(p0, d[1]), dd_mul(a0, d[2])))
    a1 = dd_div(rz1, pq1)
    z0 = dd_sub(b, dd_mul(a1, p0))
    z1 = dd_sub(a0, dd_mul(a1, dd_sub(a0, p0)))
    z2 = dd_mul(a1, a0)
    rz2 = dd_mul(z2, dd_add(dd_add(dd_mul(z0, m[2]), dd_mul(z1, m[3])), dd_mul(z2, m[4])))
    be = dd_div(rz2, rz1)
    q0 = dd_add(z0, dd_mul(be, p0))
    q1 = dd_add(z1, dd_mul(be, a0))
    pq2 = dd_mul(z2, dd_add(dd_add(dd_mul(q0, d[2]), dd_mul(q1, d[3])), dd_mul(z2, d[4])))
    a2 = dd_div(rz2, pq2)
    xs = [
        dd_add(dd_add(a0, dd_mul(a1, p0)), dd_mul(a2, q0)),
        dd_add(dd_mul(a1, a0), dd_mul(a2, q1)),
        dd_mul(a2, z2),
    ]
    rs = [
        dd_sub(z0, dd_mul(a2, q0)),
        dd_sub(z1, dd_mul(a2, dd_sub(q1, q0))),
        dd_sub(z2, dd_mul(a2, dd_sub(z2, q1))),
        dd_mul(a2, z2),
    ]
    return [x[0] for x in xs], [r[0] for r in rs]


def faces(block):
    lane = iota((8, CZ), 1)
    group = ((lane + 4) // 8) % 16
    out = jnp.zeros((8, CZ), F32)
    for k in range(16):
        x, half = k // 2, k % 2
        tile = block[x, 8 * half : 8 * half + 8, :]
        out = jnp.where(group == k, pltpu.roll(tile, 8 * k, 1) if k else tile, out)
    return out


def spread_faces(plus, minus, out):
    lane = iota((8, CZ), 1)
    low = lane % 8 < 4
    upper = iota((8, CZ), 0) < 4
    keep = (lane < 4) | (lane >= 124)
    packs = {}
    for dx in (-1, 0, 1):
        for dy in (-1, 0, 1):
            i = (dx + 1) * 3 + dy + 1
            packs[dx, dy] = jnp.where(low, plus[i], minus[i])

    def moved(tile, k):
        return pltpu.roll(tile, CZ - 8 * k, 1) if k else tile

    for xp in range(EX):
        dx, x = (0, xp) if xp < 8 else ((1, xp - 8) if xp < 12 else (-1, xp - 8))
        for half in range(2):
            out[xp, 8 * half : 8 * half + 8, :] = jnp.where(keep, moved(packs[dx, 0], 2 * x + half), 0.0)
        both = jnp.where(upper, moved(packs[dx, 1], 2 * x), moved(packs[dx, -1], 2 * x + 1))
        out[xp, 16:24, :] = jnp.where(keep, both, 0.0)


def smooth_zy(m, a):
    lane = iota(m.shape, 1)
    first, last = lane == 0, lane == CZ - 1
    rm, ra = pltpu.roll(m, 1, 1), pltpu.roll(a, 1, 1)
    lm, la = pltpu.roll(m, CZ - 1, 1), pltpu.roll(a, CZ - 1, 1)
    m = m + 0.5 * (jnp.where(first, ra, rm) + jnp.where(last, la, lm))
    a = a + 0.5 * (jnp.where(first, rm, ra) + jnp.where(last, lm, la))

    def along_y(v):
        return v + 0.5 * (pltpu.roll(v, 1, 0) + pltpu.roll(v, EY - 1, 0))

    return along_y(m), along_y(a)


def kernel(
    owner_ref, dest_ref, prior_ref, h_ref, heat_ref,
    temp_out, resid_out, added_out,
    added, prior, owner_v, dest_v, heat, hown, hm, ha, xm, ha_plus, ha_minus, xa, xa_plus, xa_minus,
    hy_plus, hy_minus, xy_plus, xy_minus, hpack, xpack, em, ea,
    send, rows, dsend, dheld, dtable, part_a, part_b, t_buf, r_buf,
    in_sem, out_sem, s1, r1, ds1, dr1, ds2, dr2, hs, hr, xs_, xr, as_, ar, bs, br,
):
    gx, gy, gz = lax.axis_index("gx"), lax.axis_index("gy"), lax.axis_index("gz")

    def at(a, b, c):
        return (lax.rem(gx + a + NX, NX), lax.rem(gy + b + NY, NY), lax.rem(gz + c + NZ, NZ))

    def remote(src, dst, ss, rs, to):
        return pltpu.make_async_remote_copy(
            src_ref=src, dst_ref=dst, send_sem=ss, recv_sem=rs, device_id=to, device_id_type=MESH
        )

    loads = [
        pltpu.make_async_copy(heat_ref, heat, in_sem.at[0]),
        pltpu.make_async_copy(h_ref, hown, in_sem.at[1]),
        pltpu.make_async_copy(prior_ref, prior, in_sem.at[2]),
        pltpu.make_async_copy(owner_ref, owner_v, in_sem.at[3]),
        pltpu.make_async_copy(dest_ref, dest_v, in_sem.at[4]),
    ]
    for c in (loads[3], loads[4], loads[0], loads[1], loads[2]):
        c.start()

    others = [(k, j, 0) for k in FAR_FIRST + [0] for j in (4, 3, 5, 2, 6, 1, 7, 0) if k or j]
    partners = others + [(0, 0, l) for l in (2, 1, 3)]
    barrier = pltpu.get_barrier_semaphore()
    for p in partners:
        pl.semaphore_signal(barrier, inc=1, device_id=at(*p), device_id_type=MESH)

    loads[3].wait()
    loads[4].wait()
    owner = owner_v[...]
    dest = dest_v[...]
    ox, oy = owner // NY, owner % NY
    kx = (ox - gx + NX) % NX
    kx = jnp.where(kx == 0, 0, jnp.where(kx <= NX // 2, 2 * kx - 1, 2 * NX - 2 * kx))
    jy = (oy - gy + NY) % NY
    rel = kx * NY + jy
    n_rows = owner.shape[1]
    named = rel == iota((NX * NY, n_rows), 0)
    earlier = (iota((n_rows, n_rows), 0) < iota((n_rows, n_rows), 1)).astype(F32).astype(BF16)
    rank = dot_nn(named.astype(F32).astype(BF16), earlier)
    rank_row = jnp.sum(jnp.where(named, rank, 0.0), axis=0, keepdims=True)
    slot = jy * CAP + rank_row.astype(jnp.int32)
    ahead = jnp.where(kx == iota((NX, n_rows), 0), (dest + 1).astype(F32), 0.0).astype(BF16)
    at_slot = (slot == iota((128, n_rows), 0)).astype(F32).astype(BF16)
    table = dot_nt(ahead, at_slot)
    dsend[...] = table.reshape(NX, 1, 128)
    dheld[0] = dsend[0]
    loads[0].wait()
    parts = three(heat[...])
    for c in range(CAP):
        mine = (named & (rank == float(c))).astype(F32).astype(BF16)
        packed = picked(mine, parts).reshape(NX, NY, CZ)
        send[:, :, c, :] = packed
        rows[0, 0, c, :] = packed[0, 0]

    pl.semaphore_wait(barrier, len(partners))

    def place(k):
        return 2 * k - 1 if k <= NX // 2 else 2 * NX - 2 * k

    for k in FAR_FIRST:
        remote(dsend.at[place(k)], dheld.at[place(k)], ds1, dr1, at(k, 0, 0)).start()
    for k, j, _ in others:
        q, i = place(k) if k else 0, int(j > 0)
        remote(send.at[q, j], rows.at[j, q], s1.at[i], r1.at[i], at(k, j, 0)).start()

    def exchange(own, wide, plus, minus, y_plus, y_minus, pack, ss, rs):
        for a, b in ((-1, 0), (1, 0), (0, -1), (0, 1), (-1, -1), (1, -1), (-1, 1), (1, 1)):
            xs = {-1: (0, 4), 0: (0, 8), 1: (4, 4)}[a]
            to = {-1: 8, 0: 0, 1: 12}[a]
            to_x = pl.ds(to, xs[1])
            from_x = pl.ds(*xs)
            if b == 0:
                remote(own.at[from_x], wide.at[to_x, pl.ds(0, CY)], ss.at[0], rs.at[0], at(a, b, 0)).start()
            elif b == -1:
                remote(own.at[from_x, pl.ds(0, 8)], y_plus.at[to_x], ss.at[1], rs.at[1], at(a, b, 0)).start()
            else:
                remote(own.at[from_x, pl.ds(8, 8)], y_minus.at[to_x], ss.at[2], rs.at[2], at(a, b, 0)).start()
        pack[...] = faces(own)
        for a in (-1, 0, 1):
            for b in (-1, 0, 1):
                i = (1 - a) * 3 + 1 - b
                remote(pack, plus.at[i], ss.at[3], rs.at[3], at(a, b, -1)).start()
                remote(pack, minus.at[i], ss.at[4], rs.at[4], at(a, b, 1)).start()

    def exchanged(wide, plus, minus, y_plus, y_minus, ss, rs):
        x_part = wide.at[pl.ds(8, 8), pl.ds(0, CY)]
        return [
            remote(v, v, ss.at[i], rs.at[i], at(1, 0, 0))
            for i, v in enumerate((x_part, y_plus, y_minus, plus, minus))
        ]

    d_along = remote(dsend.at[pl.ds(1, NX - 1)], dheld.at[pl.ds(1, NX - 1)], ds1, dr1, at(1, 0, 0))
    d_along.wait_recv()
    for j in range(1, NY):
        remote(dheld, dtable.at[j], ds2, dr2, at(0, j, 0)).start()

    d_across = remote(dtable.at[pl.ds(1, NY - 1)], dtable.at[pl.ds(1, NY - 1)], ds2, dr2, at(0, 1, 0))
    d_across.wait_recv()
    dtable[0] = dheld[...]

    loads[1].wait()
    exchange(hown, hm, ha_plus, ha_minus, hy_plus, hy_minus, hpack, hs, hr)
    hm[0:CX, 0:CY, :] = hown[...]

    places = dtable[...].reshape(NY * NX, 128)
    own_lanes = iota((NY * NX, 128), 1) // CAP == iota((NY * NX, 128), 0) // NX
    places = jnp.where(own_lanes, places, 0.0).astype(BF16)
    cell = (iota((CX * CY, 128), 0) + 1).astype(F32)
    landing = []
    for c in range(CAP):
        lanes = (iota((CX * CY, 128), 1) % CAP == c).astype(F32).astype(BF16)
        landing.append((dot_nt(lanes, places) == cell).astype(F32).astype(BF16))
    landing = jnp.concatenate(landing, axis=1)

    came = [
        remote(rows.at[0, pl.ds(1, NX - 1)], rows.at[0, pl.ds(1, NX - 1)], s1.at[0], r1.at[0], at(1, 0, 0)),
        remote(rows.at[pl.ds(1, NY - 1)], rows.at[pl.ds(1, NY - 1)], s1.at[1], r1.at[1], at(0, 1, 0)),
    ]
    for w in came:
        w.wait_recv()
    arrived = jnp.concatenate([rows[:, :, c, :].reshape(NY * NX, CZ) for c in range(CAP)], axis=0)
    added[...] = picked(landing, three(arrived)).reshape(CX, CY, CZ)
    loads[2].wait()
    prior[...] = prior[...] + added[...]

    exchange(prior, xm, xa_plus, xa_minus, xy_plus, xy_minus, xpack, xs_, xr)
    added_copy = pltpu.make_async_copy(added, added_out, out_sem.at[0])
    added_copy.start()
    xm[0:CX, 0:CY, :] = prior[...]

    h_waits = exchanged(hm, ha_plus, ha_minus, hy_plus, hy_minus, hs, hr)
    for w in h_waits:
        w.wait_recv()
    spread_faces(ha_plus, ha_minus, ha)
    upper = iota((EX, 8, CZ), 1) < 4
    hm[:, CY:EY, :] = jnp.where(upper, hy_plus[...], hy_minus[...])

    def inside(i, n):
        return (i < n - 1).astype(F32), (i > 0).astype(F32)

    (x_hi, x_lo), (y_hi, y_lo), (z_hi, z_lo) = inside(gx, NX), inside(gy, NY), inside(gz, NZ)
    row = iota((EY, CZ), 0)
    y_mask = jnp.where(row < CY, 1.0, jnp.where(row < CY + 4, y_hi, y_lo))
    z_mask = jnp.where(iota((EY, CZ), 1) < CZ // 2, z_hi, z_lo)
    for xp in range(EX):
        scale = y_mask if xp < CX else y_mask * (x_hi if xp < 12 else x_lo)
        h0 = hm[xp] * scale
        h1 = ha[xp] * (scale * z_mask)
        hm[xp] = h0
        ha[xp] = h1
        em[xp] = h0 * h0 / (1.0 + 10.5 * h0)
        ea[xp] = h1 * h1 / (1.0 + 10.5 * h1)

    x_waits = exchanged(xm, xa_plus, xa_minus, xy_plus, xy_minus, xs_, xr)
    for w in x_waits:
        w.wait_recv()
    spread_faces(xa_plus, xa_minus, xa)
    xm[:, CY:EY, :] = jnp.where(upper, xy_plus[...], xy_minus[...])

    def cells(width):
        return list(range(CX + width)) + list(range(EX - width, EX))

    def filtered(m, a, width):
        t = {x: smooth_zy(m[x], a[x]) for x in cells(width + 1)}
        out = {}
        for x in cells(width):
            lo, mid, hi = t[(x - 1) % EX], t[x], t[(x + 1) % EX]
            out[x] = tuple(mid[i] + 0.5 * (lo[i] + hi[i]) for i in range(2))
        return out

    m = {x: xm[x] * hm[x] for x in range(EX)}
    a = {x: xa[x] * ha[x] for x in range(EX)}
    us, gs = [], []
    for step in range(4):
        width = 3 - step
        t = filtered(m, a, width)
        um, ua = {}, {}
        for x in cells(width):
            um[x] = t[x][0] - m[x]
            ua[x] = t[x][1] - a[x]
            if step == 0:
                um[x] = um[x] - 10.5 * xm[x]
                ua[x] = ua[x] - 10.5 * xa[x]
        m = {x: em[x] * um[x] for x in cells(width)}
        a = {x: ea[x] * ua[x] for x in cells(width)}
        us.append([um[x][0:CY] for x in range(CX)])
        gs.append([m[x][0:CY] for x in range(CX)])

    us = [[halves(u) + (u,) for u in v] for v in us]
    gs_s = [[halves(g) + (g,) for g in v] for v in gs[:3]]
    row8 = iota((8, CZ), 0)
    lane8 = iota((8, CZ), 1)

    def pair_add(p, q):
        s, e = two_sum(p[0], q[0])
        return s, e + (p[1] + q[1])

    high, rest = jnp.zeros((8, CZ), F32), jnp.zeros((8, CZ), F32)
    for k, (i, j) in enumerate(((0, 0), (0, 1), (1, 1), (1, 2), (2, 2), (2, 3))):
        terms = []
        for x in range(CX):
            p, e = two_prod(gs_s[i][x][2], us[j][x][2], gs_s[i][x][:2], us[j][x][:2])
            terms += [(p[0:8], e[0:8]), (p[8:16], e[8:16])]
        v = tree(terms, pair_add)
        for shift in (4, 2, 1):
            v = pair_add(v, tuple(pltpu.roll(w, shift, 0) for w in v))
        high, rest = jnp.where(row8 == k, v[0], high), jnp.where(row8 == k, v[1], rest)
    v = high, rest
    for shift in (64, 32, 16, 8, 4, 2, 1):
        v = pair_add(v, tuple(pltpu.roll(w, shift, 1) for w in v))
    v = jnp.where(lane8 == row8, v[0], jnp.where(lane8 == row8 + 64, v[1], 0.0))
    part_a[0] = jnp.sum(v, axis=0, keepdims=True)

    def all_of(buf, n):
        v = buf[...].reshape(n, CZ)
        v = tree([(v[8 * i : 8 * i + 8], jnp.zeros((8, CZ), F32)) for i in range(n // 8)], pair_add)
        for shift in (4, 2, 1):
            v = pair_add(v, tuple(pltpu.roll(w, shift, 0) for w in v))
        v = v[0] + pltpu.roll(jnp.where(lane8 < 64, v[1], 0.0), 64, 1)
        return v[0:1]

    for l in (2, 1, 3, 0):
        for j in (4, 3, 5, 2, 6, 1, 7, 0):
            if j or l:
                remote(part_a.at[0], part_a.at[j * NZ + l], as_, ar, at(0, j, l)).start()
    a_all = remote(part_a.at[pl.ds(1, NY * NZ - 1)], part_a.at[pl.ds(1, NY * NZ - 1)], as_, ar, at(0, 1, 0))
    a_all.wait_recv()
    part_b[0] = all_of(part_a, NY * NZ)
    for k in FAR_FIRST:
        remote(part_b.at[0], part_b.at[k], bs, br, at(k, 0, 0)).start()
    b_all = remote(part_b.at[pl.ds(1, NX - 1)], part_b.at[pl.ds(1, NX - 1)], bs, br, at(1, 0, 0))
    b_all.wait_recv()
    s = all_of(part_b, NX)
    moments = [quick_sum(s[:, k : k + 1], s[:, 64 + k : 65 + k]) for k in range(6)]

    xs, rs = coefficients(moments)
    xs = [jnp.broadcast_to(c, (CY, CZ)) for c in xs]
    rs = [jnp.broadcast_to(c, (CY, CZ)) for c in rs]
    for x in range(CX):
        t_buf[x] = xs[0] * gs[0][x] + xs[1] * gs[1][x] + xs[2] * gs[2][x]
        r_buf[x] = (rs[0] * gs[0][x] + rs[1] * gs[1][x]) + (rs[2] * gs[2][x] + rs[3] * gs[3][x])
    outs = [
        pltpu.make_async_copy(t_buf, temp_out, out_sem.at[1]),
        pltpu.make_async_copy(r_buf, resid_out, out_sem.at[2]),
    ]
    for c in outs:
        c.start()
    for w in [d_along] + came + h_waits + x_waits + [a_all, b_all]:
        w.wait_send()
    for j in range(1, NY):
        remote(dheld, dtable.at[j], ds2, dr2, at(0, j, 0)).wait_send()
    added_copy.wait()
    for c in outs:
        c.wait()


def local(prior, h, heat, owner, dest):
    n = dest.shape[0]
    hbm = pl.BlockSpec(memory_space=pltpu.HBM)
    block = jax.ShapeDtypeStruct((CX, CY, CZ), F32)
    V = lambda *shape: pltpu.VMEM(shape, F32)
    D = pltpu.SemaphoreType.DMA
    wide = V(EX, EY, CZ)
    nine, ys, tile = V(9, 8, CZ), V(EX, 8, CZ), V(8, CZ)
    own = V(CX, CY, CZ)
    scratch = [
        own, own, pltpu.VMEM((1, n), jnp.int32), pltpu.VMEM((1, n), jnp.int32), V(n, CZ), own, wide, wide, wide, nine, nine, wide, nine, nine,
        ys, ys, ys, ys, tile, tile, wide, wide,
        V(NX, NY, CAP, CZ), V(NY, NX, CAP, CZ),
        V(NX, 1, 128), V(NX, 1, 128), V(NY, NX, 1, 128),
        V(NY * NZ, 1, CZ), V(NX, 1, CZ), own, own,
        D((5,)), D((3,)), D((2,)), D((2,)), D, D, D, D,
        D((5,)), D((5,)), D((5,)), D((5,)), D, D, D, D,
    ]
    step, rest, added = pl.pallas_call(
        kernel,
        out_shape=(block, block, block),
        in_specs=[hbm] * 5,
        out_specs=(hbm,) * 3,
        scratch_shapes=scratch,
        compiler_params=pltpu.CompilerParams(
            collective_id=0, has_side_effects=True, vmem_limit_bytes=VMEM_BYTES
        ),
    )(owner.reshape(1, n), dest.reshape(1, n), prior, h, heat)
    deposited = prior + added
    over = 1.0 / h
    return deposited + step * over, rest * (over + 10.5), deposited


def solution(mesh):
    placed = (
        P("gx", "gy", "gz"),
        P("gx", "gy", "gz"),
        P(("gx", "gy"), "gz"),
        P(("gx", "gy"), None),
        P(("gx", "gy")),
    )
    return jax.shard_map(
        local,
        mesh=mesh,
        in_specs=placed,
        out_specs=(P("gx", "gy", "gz"), P("gx", "gy", "gz"), P("gx", "gy", "gz")),
        check_vma=False,
    )
```

```python
import jax
import jax.numpy as jnp
from jax import lax
from jax.experimental import pallas as pl
from jax.experimental.pallas import tpu as pltpu
from jax.sharding import PartitionSpec as P

MESH = pl.DeviceIdType.MESH
F32 = jnp.float32
BF16 = jnp.bfloat16
NX, NY, NZ = 16, 8, 4
CX, CY, CZ = 8, 16, 128
EX, EY = 16, 24
CAP = 4
VMEM_BYTES = 54992 * 1024
FAR = [8, 7, 9, 6, 10, 5, 11]
CLOSE = [4, 12, 3, 13, 2, 14, 1, 15]
REACH = 4
AROUND = [(a, b, c) for a in (-1, 0, 1) for b in (-1, 0, 1) for c in (-1, 0, 1) if (a, b, c) != (0, 0, 0)]


def iota(shape, dim):
    return lax.broadcasted_iota(jnp.int32, shape, dim)


def dot_nn(a, b):
    return lax.dot_general(a, b, (((1,), (0,)), ((), ())), preferred_element_type=F32)


def dot_nt(a, b):
    return lax.dot_general(a, b, (((1,), (1,)), ((), ())), preferred_element_type=F32)


def three(v):
    hi = v.astype(BF16)
    rest = v - hi.astype(F32)
    mid = rest.astype(BF16)
    low = (rest - mid.astype(F32)).astype(BF16)
    return jnp.concatenate([hi, mid, low], axis=1)


def picked(onehot, parts):
    out = dot_nn(onehot, parts)
    n = out.shape[1] // 3
    return (out[:, 2 * n :] + out[:, n : 2 * n]) + out[:, :n]


def two_sum(a, b):
    s = a + b
    t = s - a
    return s, (a - (s - t)) + (b - t)


def quick_sum(a, b):
    s = a + b
    return s, b - (s - a)


def halves(a):
    c = a * 4097.0
    hi = c - (c - a)
    return hi, a - hi


def two_prod(a, b, sa=None, sb=None):
    p = a * b
    ah, al = halves(a) if sa is None else sa
    bh, bl = halves(b) if sb is None else sb
    return p, ((ah * bh - p) + ah * bl + al * bh) + al * bl


def dd_add(a, b):
    s, e = two_sum(a[0], b[0])
    return quick_sum(s, e + (a[1] + b[1]))


def dd_neg(a):
    return -a[0], -a[1]


def dd_sub(a, b):
    return dd_add(a, dd_neg(b))


def dd_mul(a, b):
    p, e = two_prod(a[0], b[0])
    return quick_sum(p, e + (a[0] * b[1] + a[1] * b[0]))


def dd_div(a, b):
    q = a[0] / b[0]
    r = dd_sub(a, dd_mul((q, jnp.zeros_like(q)), b))
    q2 = r[0] / b[0]
    return quick_sum(q, q2)


def tree(values, add):
    while len(values) > 1:
        values = [add(*values[i : i + 2]) if i + 1 < len(values) else values[i] for i in range(0, len(values), 2)]
    return values[0]


def coefficients(m):
    d = [dd_sub(m[k], m[k + 1]) for k in range(5)]
    one = (jnp.ones_like(m[0][0]), jnp.zeros_like(m[0][0]))
    a0 = dd_div(m[0], d[0])
    b = dd_sub(one, a0)
    rz1 = dd_mul(a0, dd_add(dd_mul(b, m[1]), dd_mul(a0, m[2])))
    p0 = dd_add(b, dd_div(rz1, m[0]))
    pq1 = dd_mul(a0, dd_add(dd_mul(p0, d[1]), dd_mul(a0, d[2])))
    a1 = dd_div(rz1, pq1)
    z0 = dd_sub(b, dd_mul(a1, p0))
    z1 = dd_sub(a0, dd_mul(a1, dd_sub(a0, p0)))
    z2 = dd_mul(a1, a0)
    rz2 = dd_mul(z2, dd_add(dd_add(dd_mul(z0, m[2]), dd_mul(z1, m[3])), dd_mul(z2, m[4])))
    be = dd_div(rz2, rz1)
    q0 = dd_add(z0, dd_mul(be, p0))
    q1 = dd_add(z1, dd_mul(be, a0))
    pq2 = dd_mul(z2, dd_add(dd_add(dd_mul(q0, d[2]), dd_mul(q1, d[3])), dd_mul(z2, d[4])))
    a2 = dd_div(rz2, pq2)
    xs = [
        dd_add(dd_add(a0, dd_mul(a1, p0)), dd_mul(a2, q0)),
        dd_add(dd_mul(a1, a0), dd_mul(a2, q1)),
        dd_mul(a2, z2),
    ]
    rs = [
        dd_sub(z0, dd_mul(a2, q0)),
        dd_sub(z1, dd_mul(a2, dd_sub(q1, q0))),
        dd_sub(z2, dd_mul(a2, dd_sub(z2, q1))),
        dd_mul(a2, z2),
    ]
    return [x[0] for x in xs], [r[0] for r in rs]


def faces(block):
    lane = iota((8, CZ), 1)
    group = ((lane + 4) // 8) % 16
    out = jnp.zeros((8, CZ), F32)
    for k in range(16):
        x, half = k // 2, k % 2
        tile = block[x, 8 * half : 8 * half + 8, :]
        out = jnp.where(group == k, pltpu.roll(tile, 8 * k, 1) if k else tile, out)
    return out


def spread_faces(plus, minus, out):
    lane = iota((8, CZ), 1)
    low = lane % 8 < 4
    upper = iota((8, CZ), 0) < 4
    keep = (lane < 4) | (lane >= 124)
    packs = {}
    for dx in (-1, 0, 1):
        for dy in (-1, 0, 1):
            i = (dx + 1) * 3 + dy + 1
            packs[dx, dy] = jnp.where(low, plus[i], minus[i])

    def moved(tile, k):
        return pltpu.roll(tile, CZ - 8 * k, 1) if k else tile

    for xp in range(EX):
        dx, x = (0, xp) if xp < 8 else ((1, xp - 8) if xp < 12 else (-1, xp - 8))
        for half in range(2):
            out[xp, 8 * half : 8 * half + 8, :] = jnp.where(keep, moved(packs[dx, 0], 2 * x + half), 0.0)
        both = jnp.where(upper, moved(packs[dx, 1], 2 * x), moved(packs[dx, -1], 2 * x + 1))
        out[xp, 16:24, :] = jnp.where(keep, both, 0.0)


def smooth_zy(m, a):
    lane = iota(m.shape, 1)
    first, last = lane == 0, lane == CZ - 1
    rm, ra = pltpu.roll(m, 1, 1), pltpu.roll(a, 1, 1)
    lm, la = pltpu.roll(m, CZ - 1, 1), pltpu.roll(a, CZ - 1, 1)
    m = m + 0.5 * (jnp.where(first, ra, rm) + jnp.where(last, la, lm))
    a = a + 0.5 * (jnp.where(first, rm, ra) + jnp.where(last, lm, la))

    def along_y(v):
        return v + 0.5 * (pltpu.roll(v, 1, 0) + pltpu.roll(v, EY - 1, 0))

    return along_y(m), along_y(a)


def kernel(
    owner_ref, dest_ref, prior_ref, h_ref, heat_ref,
    t_buf, r_buf, added,
    prior, owner_v, dest_v, heat, hown, hm, ha, xm, ha_plus, ha_minus, xa, xa_plus, xa_minus,
    hy_plus, hy_minus, xy_plus, xy_minus, hpack, xpack, em, ea,
    send, rows, dsend, dheld, dtable, part_a, part_b,
    in_sem, s1, r1, ds1, dr1, ds2, dr2, hs, hr, xs_, xr, as_, ar, bs, br,
):
    gx, gy, gz = lax.axis_index("gx"), lax.axis_index("gy"), lax.axis_index("gz")

    def at(a, b, c):
        return (lax.rem(gx + a + NX, NX), lax.rem(gy + b + NY, NY), lax.rem(gz + c + NZ, NZ))

    def remote(src, dst, ss, rs, to):
        return pltpu.make_async_remote_copy(
            src_ref=src, dst_ref=dst, send_sem=ss, recv_sem=rs, device_id=to, device_id_type=MESH
        )

    loads = [
        pltpu.make_async_copy(heat_ref, heat, in_sem.at[0]),
        pltpu.make_async_copy(h_ref, hown, in_sem.at[1]),
        pltpu.make_async_copy(prior_ref, prior, in_sem.at[2]),
        pltpu.make_async_copy(owner_ref, owner_v, in_sem.at[3]),
        pltpu.make_async_copy(dest_ref, dest_v, in_sem.at[4]),
    ]
    for c in (loads[3], loads[4], loads[0], loads[1], loads[2]):
        c.start()

    def group(ks):
        return [(k, j, 0) for k in ks for j in (4, 3, 5, 2, 6, 1, 7, 0) if k or j]

    others = group(FAR + CLOSE + [0])
    partners = others + [(0, 0, 2)] + [(0, 0, 1), (0, 0, 3)]
    barrier = pltpu.get_barrier_semaphore()
    for p in partners:
        pl.semaphore_signal(barrier, inc=1, device_id=at(*p), device_id_type=MESH)

    loads[3].wait()
    loads[4].wait()
    owner = owner_v[...]
    dest = dest_v[...]
    ox, oy = owner // NY, owner % NY
    kx = (ox - gx + NX) % NX
    kx = jnp.where(kx == 0, 0, jnp.where(kx <= NX // 2, 2 * kx - 1, 2 * NX - 2 * kx))
    jy = (oy - gy + NY) % NY
    rel = kx * NY + jy
    n_rows = owner.shape[1]
    named = rel == iota((NX * NY, n_rows), 0)
    earlier = (iota((n_rows, n_rows), 0) < iota((n_rows, n_rows), 1)).astype(F32).astype(BF16)
    rank = dot_nn(named.astype(F32).astype(BF16), earlier)
    rank_row = jnp.sum(jnp.where(named, rank, 0.0), axis=0, keepdims=True)
    slot = jy * CAP + rank_row.astype(jnp.int32)
    ahead = jnp.where(kx == iota((NX, n_rows), 0), (dest + 1).astype(F32), 0.0).astype(BF16)
    at_slot = (slot == iota((128, n_rows), 0)).astype(F32).astype(BF16)
    table = dot_nt(ahead, at_slot)
    dsend[...] = table.reshape(NX, 1, 128)
    dheld[0] = dsend[0]
    loads[0].wait()
    parts = three(heat[...])
    for c in range(CAP):
        mine = (named & (rank == float(c))).astype(F32).astype(BF16)
        packed = picked(mine, parts).reshape(NX, NY, CZ)
        send[:, :, c, :] = packed
        rows[0, 0, c, :] = packed[0, 0]

    loads[1].wait()
    hpack[...] = faces(hown)

    pl.semaphore_wait(barrier, len(partners))
    def exchange(own, wide, plus, minus, y_plus, y_minus, pack, ss, rs):
        for a, b in ((-1, 0), (1, 0), (0, -1), (0, 1), (-1, -1), (1, -1), (-1, 1), (1, 1)):
            xs = {-1: (0, 4), 0: (0, 8), 1: (4, 4)}[a]
            to = {-1: 8, 0: 0, 1: 12}[a]
            to_x = pl.ds(to, xs[1])
            from_x = pl.ds(*xs)
            if b == 0:
                remote(own.at[from_x], wide.at[to_x, pl.ds(0, CY)], ss.at[0], rs.at[0], at(a, b, 0)).start()
            elif b == -1:
                remote(own.at[from_x, pl.ds(0, 8)], y_plus.at[to_x], ss.at[1], rs.at[1], at(a, b, 0)).start()
            else:
                remote(own.at[from_x, pl.ds(8, 8)], y_minus.at[to_x], ss.at[2], rs.at[2], at(a, b, 0)).start()
        for a in (-1, 0, 1):
            for b in (-1, 0, 1):
                i = (1 - a) * 3 + 1 - b
                remote(pack, plus.at[i], ss.at[3], rs.at[3], at(a, b, -1)).start()
                remote(pack, minus.at[i], ss.at[4], rs.at[4], at(a, b, 1)).start()

    def exchanged(wide, plus, minus, y_plus, y_minus, ss, rs):
        x_part = wide.at[pl.ds(8, 8), pl.ds(0, CY)]
        return [
            remote(v, v, ss.at[i], rs.at[i], at(1, 0, 0))
            for i, v in enumerate((x_part, y_plus, y_minus, plus, minus))
        ]


    def place(k):
        return 2 * k - 1 if k <= NX // 2 else 2 * NX - 2 * k

    def send_rows(ks):
        for k in ks:
            if k:
                remote(dsend.at[place(k)], dheld.at[place(k)], ds1, dr1, at(k, 0, 0)).start()
        for k, j, _ in group(ks):
            q, i = place(k) if k else 0, int(j > 0)
            remote(send.at[q, j], rows.at[j, q], s1.at[i], r1.at[i], at(k, j, 0)).start()

    send_rows(FAR + CLOSE + [0])

    d_along = remote(dsend.at[pl.ds(1, NX - 1)], dheld.at[pl.ds(1, NX - 1)], ds1, dr1, at(1, 0, 0))
    d_along.wait_recv()
    for j in range(1, NY):
        remote(dheld, dtable.at[j], ds2, dr2, at(0, j, 0)).start()

    d_across = remote(dtable.at[pl.ds(1, NY - 1)], dtable.at[pl.ds(1, NY - 1)], ds2, dr2, at(0, 1, 0))
    d_across.wait_recv()
    dtable[0] = dheld[...]
    exchange(hown, hm, ha_plus, ha_minus, hy_plus, hy_minus, hpack, hs, hr)
    hm[0:CX, 0:CY, :] = hown[...]
    places = dtable[...].reshape(NY * NX, 128)
    own_lanes = iota((NY * NX, 128), 1) // CAP == iota((NY * NX, 128), 0) // NX
    places = jnp.where(own_lanes, places, 0.0).astype(BF16)
    cell = (iota((CX * CY, 128), 0) + 1).astype(F32)
    landing = []
    for c in range(CAP):
        lanes = (iota((CX * CY, 128), 1) % CAP == c).astype(F32).astype(BF16)
        landing.append((dot_nt(lanes, places) == cell).astype(F32).astype(BF16))
    landing = jnp.concatenate(landing, axis=1)

    came = [
        remote(rows.at[0, pl.ds(1, NX - 1)], rows.at[0, pl.ds(1, NX - 1)], s1.at[0], r1.at[0], at(1, 0, 0)),
        remote(rows.at[pl.ds(1, NY - 1)], rows.at[pl.ds(1, NY - 1)], s1.at[1], r1.at[1], at(0, 1, 0)),
    ]
    for w in came:
        w.wait_recv()
    arrived = jnp.concatenate([rows[:, :, c, :].reshape(NY * NX, CZ) for c in range(CAP)], axis=0)
    added[...] = picked(landing, three(arrived)).reshape(CX, CY, CZ)
    loads[2].wait()
    prior[...] = prior[...] + added[...]

    xpack[...] = faces(prior)
    exchange(prior, xm, xa_plus, xa_minus, xy_plus, xy_minus, xpack, xs_, xr)
    xm[0:CX, 0:CY, :] = prior[...]

    h_waits = exchanged(hm, ha_plus, ha_minus, hy_plus, hy_minus, hs, hr)
    for w in h_waits:
        w.wait_recv()
    spread_faces(ha_plus, ha_minus, ha)
    upper = iota((EX, 8, CZ), 1) < 4
    hm[:, CY:EY, :] = jnp.where(upper, hy_plus[...], hy_minus[...])

    def inside(i, n):
        return (i < n - 1).astype(F32), (i > 0).astype(F32)

    (x_hi, x_lo), (y_hi, y_lo), (z_hi, z_lo) = inside(gx, NX), inside(gy, NY), inside(gz, NZ)
    row = iota((EY, CZ), 0)
    y_mask = jnp.where(row < CY, 1.0, jnp.where(row < CY + 4, y_hi, y_lo))
    z_mask = jnp.where(iota((EY, CZ), 1) < CZ // 2, z_hi, z_lo)
    for xp in range(EX):
        scale = y_mask if xp < CX else y_mask * (x_hi if xp < 12 else x_lo)
        h0 = hm[xp] * scale
        h1 = ha[xp] * (scale * z_mask)
        hm[xp] = h0
        ha[xp] = h1
        em[xp] = h0 * h0 / (1.0 + 10.5 * h0)
        ea[xp] = h1 * h1 / (1.0 + 10.5 * h1)

    x_waits = exchanged(xm, xa_plus, xa_minus, xy_plus, xy_minus, xs_, xr)
    for w in x_waits:
        w.wait_recv()
    spread_faces(xa_plus, xa_minus, xa)
    xm[:, CY:EY, :] = jnp.where(upper, xy_plus[...], xy_minus[...])

    def cells(width):
        return list(range(CX + width)) + list(range(EX - width, EX))

    def filtered(m, a, width):
        t = {x: smooth_zy(m[x], a[x]) for x in cells(width + 1)}
        out = {}
        for x in cells(width):
            lo, mid, hi = t[(x - 1) % EX], t[x], t[(x + 1) % EX]
            out[x] = tuple(mid[i] + 0.5 * (lo[i] + hi[i]) for i in range(2))
        return out

    m = {x: xm[x] * hm[x] for x in range(EX)}
    a = {x: xa[x] * ha[x] for x in range(EX)}
    us, gs = [], []
    for step in range(4):
        width = 3 - step
        t = filtered(m, a, width)
        um, ua = {}, {}
        for x in cells(width):
            um[x] = t[x][0] - m[x]
            ua[x] = t[x][1] - a[x]
            if step == 0:
                um[x] = um[x] - 10.5 * xm[x]
                ua[x] = ua[x] - 10.5 * xa[x]
        m = {x: em[x] * um[x] for x in cells(width)}
        a = {x: ea[x] * ua[x] for x in cells(width)}
        us.append([um[x][0:CY] for x in range(CX)])
        gs.append([m[x][0:CY] for x in range(CX)])

    us = [[halves(u) + (u,) for u in v] for v in us]
    gs_s = [[halves(g) + (g,) for g in v] for v in gs[:3]]
    row8 = iota((8, CZ), 0)
    lane8 = iota((8, CZ), 1)

    def pair_add(p, q):
        s, e = two_sum(p[0], q[0])
        return s, e + (p[1] + q[1])

    high, rest = jnp.zeros((8, CZ), F32), jnp.zeros((8, CZ), F32)
    for k, (i, j) in enumerate(((0, 0), (0, 1), (1, 1), (1, 2), (2, 2), (2, 3))):
        terms = []
        for x in range(CX):
            p, e = two_prod(gs_s[i][x][2], us[j][x][2], gs_s[i][x][:2], us[j][x][:2])
            terms += [(p[0:8], e[0:8]), (p[8:16], e[8:16])]
        v = tree(terms, pair_add)
        for shift in (4, 2, 1):
            v = pair_add(v, tuple(pltpu.roll(w, shift, 0) for w in v))
        high, rest = jnp.where(row8 == k, v[0], high), jnp.where(row8 == k, v[1], rest)
    v = high, rest
    for shift in (64, 32, 16, 8, 4, 2, 1):
        v = pair_add(v, tuple(pltpu.roll(w, shift, 1) for w in v))
    v = jnp.where(lane8 == row8, v[0], jnp.where(lane8 == row8 + 64, v[1], 0.0))
    part_a[0] = jnp.sum(v, axis=0, keepdims=True)

    def all_of(buf, n):
        v = buf[...].reshape(n, CZ)
        v = tree([(v[8 * i : 8 * i + 8], jnp.zeros((8, CZ), F32)) for i in range(n // 8)], pair_add)
        for shift in (4, 2, 1):
            v = pair_add(v, tuple(pltpu.roll(w, shift, 0) for w in v))
        v = v[0] + pltpu.roll(jnp.where(lane8 < 64, v[1], 0.0), 64, 1)
        return v[0:1]

    for l in (2, 1, 3, 0):
        for j in (4, 3, 5, 2, 6, 1, 7, 0):
            if j or l:
                remote(part_a.at[0], part_a.at[j * NZ + l], as_, ar, at(0, j, l)).start()
    a_all = remote(part_a.at[pl.ds(1, NY * NZ - 1)], part_a.at[pl.ds(1, NY * NZ - 1)], as_, ar, at(0, 1, 0))
    a_all.wait_recv()
    part_b[0] = all_of(part_a, NY * NZ)
    for k in FAR + CLOSE:
        remote(part_b.at[0], part_b.at[k], bs, br, at(k, 0, 0)).start()
    b_all = remote(part_b.at[pl.ds(1, NX - 1)], part_b.at[pl.ds(1, NX - 1)], bs, br, at(1, 0, 0))
    b_all.wait_recv()
    s = all_of(part_b, NX)
    moments = [quick_sum(s[:, k : k + 1], s[:, 64 + k : 65 + k]) for k in range(6)]

    xs, rs = coefficients(moments)
    xs = [jnp.broadcast_to(c, (CY, CZ)) for c in xs]
    rs = [jnp.broadcast_to(c, (CY, CZ)) for c in rs]
    for x in range(CX):
        t_buf[x] = xs[0] * gs[0][x] + xs[1] * gs[1][x] + xs[2] * gs[2][x]
        r_buf[x] = (rs[0] * gs[0][x] + rs[1] * gs[1][x]) + (rs[2] * gs[2][x] + rs[3] * gs[3][x])
    for w in [d_along] + came + h_waits + x_waits + [a_all, b_all]:
        w.wait_send()
    for j in range(1, NY):
        remote(dheld, dtable.at[j], ds2, dr2, at(0, j, 0)).wait_send()


def local(prior, h, heat, owner, dest):
    n = dest.shape[0]
    vmem = pl.BlockSpec(memory_space=pltpu.VMEM)
    hbm = pl.BlockSpec(memory_space=pltpu.HBM)
    block = jax.ShapeDtypeStruct((CX, CY, CZ), F32)
    V = lambda *shape: pltpu.VMEM(shape, F32)
    D = pltpu.SemaphoreType.DMA
    wide = V(EX, EY, CZ)
    nine, ys, tile = V(9, 8, CZ), V(EX, 8, CZ), V(8, CZ)
    own = V(CX, CY, CZ)
    scratch = [
        own, pltpu.VMEM((1, n), jnp.int32), pltpu.VMEM((1, n), jnp.int32), V(n, CZ), own, wide, wide, wide, nine, nine, wide, nine, nine,
        ys, ys, ys, ys, tile, tile, wide, wide,
        V(NX, NY, CAP, CZ), V(NY, NX, CAP, CZ),
        V(NX, 1, 128), V(NX, 1, 128), V(NY, NX, 1, 128),
        V(NY * NZ, 1, CZ), V(NX, 1, CZ),
        D((5,)), D((2,)), D((2,)), D, D, D, D,
        D((5,)), D((5,)), D((5,)), D((5,)), D, D, D, D,
    ]
    step, rest, added = pl.pallas_call(
        kernel,
        out_shape=(block, block, block),
        in_specs=[hbm] * 5,
        out_specs=(vmem,) * 3,
        scratch_shapes=scratch,
        compiler_params=pltpu.CompilerParams(
            collective_id=0, has_side_effects=True, vmem_limit_bytes=VMEM_BYTES
        ),
    )(owner.reshape(1, n), dest.reshape(1, n), prior, h, heat)
    deposited = prior + added
    over = 1.0 / h
    return deposited + step * over, rest * (over + 10.5), deposited


def solution(mesh):
    placed = (
        P("gx", "gy", "gz"),
        P("gx", "gy", "gz"),
        P(("gx", "gy"), "gz"),
        P(("gx", "gy"), None),
        P(("gx", "gy")),
    )
    return jax.shard_map(
        local,
        mesh=mesh,
        in_specs=placed,
        out_specs=(P("gx", "gy", "gz"), P("gx", "gy", "gz"), P("gx", "gy", "gz")),
        check_vma=False,
    )
```

```python
import jax
import jax.numpy as jnp
from jax import lax
from jax.experimental import pallas as pl
from jax.experimental.pallas import tpu as pltpu
from jax.sharding import PartitionSpec as P

MESH = pl.DeviceIdType.MESH
F32 = jnp.float32
BF16 = jnp.bfloat16
NX, NY, NZ = 16, 8, 4
CX, CY, CZ = 8, 16, 128
EX, EY = 16, 24
CAP = 4
VMEM_BYTES = 54992 * 1024
FAR = [8, 7, 9, 6, 10, 5, 11]
CLOSE = [4, 12, 3, 13, 2, 14, 1, 15]
REACH = 4
AROUND = [(a, b, c) for a in (-1, 0, 1) for b in (-1, 0, 1) for c in (-1, 0, 1) if (a, b, c) != (0, 0, 0)]


def iota(shape, dim):
    return lax.broadcasted_iota(jnp.int32, shape, dim)


def dot_nn(a, b):
    return lax.dot_general(a, b, (((1,), (0,)), ((), ())), preferred_element_type=F32)


def dot_nt(a, b):
    return lax.dot_general(a, b, (((1,), (1,)), ((), ())), preferred_element_type=F32)


def three(v):
    hi = v.astype(BF16)
    rest = v - hi.astype(F32)
    mid = rest.astype(BF16)
    low = (rest - mid.astype(F32)).astype(BF16)
    return jnp.concatenate([hi, mid, low], axis=1)


def picked(onehot, parts):
    out = dot_nn(onehot, parts)
    n = out.shape[1] // 3
    return (out[:, 2 * n :] + out[:, n : 2 * n]) + out[:, :n]


def two_sum(a, b):
    s = a + b
    t = s - a
    return s, (a - (s - t)) + (b - t)


def quick_sum(a, b):
    s = a + b
    return s, b - (s - a)


def halves(a):
    c = a * 4097.0
    hi = c - (c - a)
    return hi, a - hi


def two_prod(a, b, sa=None, sb=None):
    p = a * b
    ah, al = halves(a) if sa is None else sa
    bh, bl = halves(b) if sb is None else sb
    return p, ((ah * bh - p) + ah * bl + al * bh) + al * bl


def dd_add(a, b):
    s, e = two_sum(a[0], b[0])
    return quick_sum(s, e + (a[1] + b[1]))


def dd_neg(a):
    return -a[0], -a[1]


def dd_sub(a, b):
    return dd_add(a, dd_neg(b))


def dd_mul(a, b):
    p, e = two_prod(a[0], b[0])
    return quick_sum(p, e + (a[0] * b[1] + a[1] * b[0]))


def dd_div(a, b):
    q = a[0] / b[0]
    r = dd_sub(a, dd_mul((q, jnp.zeros_like(q)), b))
    q2 = r[0] / b[0]
    return quick_sum(q, q2)


def tree(values, add):
    while len(values) > 1:
        values = [add(*values[i : i + 2]) if i + 1 < len(values) else values[i] for i in range(0, len(values), 2)]
    return values[0]


def coefficients(m):
    d = [dd_sub(m[k], m[k + 1]) for k in range(5)]
    one = (jnp.ones_like(m[0][0]), jnp.zeros_like(m[0][0]))
    a0 = dd_div(m[0], d[0])
    b = dd_sub(one, a0)
    rz1 = dd_mul(a0, dd_add(dd_mul(b, m[1]), dd_mul(a0, m[2])))
    p0 = dd_add(b, dd_div(rz1, m[0]))
    pq1 = dd_mul(a0, dd_add(dd_mul(p0, d[1]), dd_mul(a0, d[2])))
    a1 = dd_div(rz1, pq1)
    z0 = dd_sub(b, dd_mul(a1, p0))
    z1 = dd_sub(a0, dd_mul(a1, dd_sub(a0, p0)))
    z2 = dd_mul(a1, a0)
    rz2 = dd_mul(z2, dd_add(dd_add(dd_mul(z0, m[2]), dd_mul(z1, m[3])), dd_mul(z2, m[4])))
    be = dd_div(rz2, rz1)
    q0 = dd_add(z0, dd_mul(be, p0))
    q1 = dd_add(z1, dd_mul(be, a0))
    pq2 = dd_mul(z2, dd_add(dd_add(dd_mul(q0, d[2]), dd_mul(q1, d[3])), dd_mul(z2, d[4])))
    a2 = dd_div(rz2, pq2)
    xs = [
        dd_add(dd_add(a0, dd_mul(a1, p0)), dd_mul(a2, q0)),
        dd_add(dd_mul(a1, a0), dd_mul(a2, q1)),
        dd_mul(a2, z2),
    ]
    rs = [
        dd_sub(z0, dd_mul(a2, q0)),
        dd_sub(z1, dd_mul(a2, dd_sub(q1, q0))),
        dd_sub(z2, dd_mul(a2, dd_sub(z2, q1))),
        dd_mul(a2, z2),
    ]
    return [x[0] for x in xs], [r[0] for r in rs]


def faces(block):
    lane = iota((8, CZ), 1)
    group = ((lane + 4) // 8) % 16
    out = jnp.zeros((8, CZ), F32)
    for k in range(16):
        x, half = k // 2, k % 2
        tile = block[x, 8 * half : 8 * half + 8, :]
        out = jnp.where(group == k, pltpu.roll(tile, 8 * k, 1) if k else tile, out)
    return out


def spread_faces(plus, minus, out):
    lane = iota((8, CZ), 1)
    low = lane % 8 < 4
    upper = iota((8, CZ), 0) < 4
    keep = (lane < 4) | (lane >= 124)
    packs = {}
    for dx in (-1, 0, 1):
        for dy in (-1, 0, 1):
            i = (dx + 1) * 3 + dy + 1
            packs[dx, dy] = jnp.where(low, plus[i], minus[i])

    def moved(tile, k):
        return pltpu.roll(tile, CZ - 8 * k, 1) if k else tile

    for xp in range(EX):
        dx, x = (0, xp) if xp < 8 else ((1, xp - 8) if xp < 12 else (-1, xp - 8))
        for half in range(2):
            out[xp, 8 * half : 8 * half + 8, :] = jnp.where(keep, moved(packs[dx, 0], 2 * x + half), 0.0)
        both = jnp.where(upper, moved(packs[dx, 1], 2 * x), moved(packs[dx, -1], 2 * x + 1))
        out[xp, 16:24, :] = jnp.where(keep, both, 0.0)


def smooth_zy(m, a):
    lane = iota(m.shape, 1)
    first, last = lane == 0, lane == CZ - 1
    rm, ra = pltpu.roll(m, 1, 1), pltpu.roll(a, 1, 1)
    lm, la = pltpu.roll(m, CZ - 1, 1), pltpu.roll(a, CZ - 1, 1)
    m = m + 0.5 * (jnp.where(first, ra, rm) + jnp.where(last, la, lm))
    a = a + 0.5 * (jnp.where(first, rm, ra) + jnp.where(last, lm, la))

    def along_y(v):
        return v + 0.5 * (pltpu.roll(v, 1, 0) + pltpu.roll(v, EY - 1, 0))

    return along_y(m), along_y(a)


def kernel(
    owner_ref, dest_ref, prior_ref, h_ref, heat_ref,
    t_buf, r_buf, added,
    prior, owner_v, dest_v, heat, hown, hm, ha, xm, ha_plus, ha_minus, xa, xa_plus, xa_minus,
    hy_plus, hy_minus, xy_plus, xy_minus, hpack, xpack, em, ea,
    send, rows, dsend, dheld, dtable, part_a, part_b,
    in_sem, s1, r1, ds1, dr1, ds2, dr2, hs, hr, xs_, xr, as_, ar, bs, br,
):
    gx, gy, gz = lax.axis_index("gx"), lax.axis_index("gy"), lax.axis_index("gz")

    def at(a, b, c):
        return (lax.rem(gx + a + NX, NX), lax.rem(gy + b + NY, NY), lax.rem(gz + c + NZ, NZ))

    def remote(src, dst, ss, rs, to):
        return pltpu.make_async_remote_copy(
            src_ref=src, dst_ref=dst, send_sem=ss, recv_sem=rs, device_id=to, device_id_type=MESH
        )

    loads = [
        pltpu.make_async_copy(heat_ref, heat, in_sem.at[0]),
        pltpu.make_async_copy(h_ref, hown, in_sem.at[1]),
        pltpu.make_async_copy(prior_ref, prior, in_sem.at[2]),
        pltpu.make_async_copy(owner_ref, owner_v, in_sem.at[3]),
        pltpu.make_async_copy(dest_ref, dest_v, in_sem.at[4]),
    ]
    for c in (loads[3], loads[4], loads[0], loads[1], loads[2]):
        c.start()

    def group(ks):
        return [(k, j, 0) for k in ks for j in (4, 3, 5, 2, 6, 1, 7, 0) if k or j]

    others = group(FAR + CLOSE + [0])
    partners = others + [(0, 0, 2)] + [(0, 0, 1), (0, 0, 3)]
    barrier = pltpu.get_barrier_semaphore()
    for p in partners:
        pl.semaphore_signal(barrier, inc=1, device_id=at(*p), device_id_type=MESH)

    loads[3].wait()
    loads[4].wait()
    owner = owner_v[...]
    dest = dest_v[...]
    ox, oy = owner // NY, owner % NY
    kx = (ox - gx + NX) % NX
    kx = jnp.where(kx == 0, 0, jnp.where(kx <= NX // 2, 2 * kx - 1, 2 * NX - 2 * kx))
    jy = (oy - gy + NY) % NY
    rel = kx * NY + jy
    n_rows = owner.shape[1]
    named = rel == iota((NX * NY, n_rows), 0)
    earlier = (iota((n_rows, n_rows), 0) < iota((n_rows, n_rows), 1)).astype(F32).astype(BF16)
    rank = dot_nn(named.astype(F32).astype(BF16), earlier)
    rank_row = jnp.sum(jnp.where(named, rank, 0.0), axis=0, keepdims=True)
    slot = jy * CAP + rank_row.astype(jnp.int32)
    ahead = jnp.where(kx == iota((NX, n_rows), 0), (dest + 1).astype(F32), 0.0).astype(BF16)
    at_slot = (slot == iota((128, n_rows), 0)).astype(F32).astype(BF16)
    table = dot_nt(ahead, at_slot)
    dsend[...] = table.reshape(NX, 1, 128)
    dheld[0] = dsend[0]
    loads[0].wait()
    parts = three(heat[...])
    for c in range(CAP):
        mine = (named & (rank == float(c))).astype(F32).astype(BF16)
        packed = picked(mine, parts).reshape(NX, NY, CZ)
        send[:, :, c, :] = packed
        rows[0, 0, c, :] = packed[0, 0]

    loads[1].wait()
    hpack[...] = faces(hown)

    pl.semaphore_wait(barrier, len(partners))
    def exchange(own, wide, plus, minus, y_plus, y_minus, pack, ss, rs, ready=None):
        for a, b in ((-1, -1), (1, -1), (-1, 1), (1, 1), (-1, 0), (1, 0), (0, -1), (0, 1)):
            xs = {-1: (0, 4), 0: (0, 8), 1: (4, 4)}[a]
            to = {-1: 8, 0: 0, 1: 12}[a]
            to_x = pl.ds(to, xs[1])
            from_x = pl.ds(*xs)
            if b == 0:
                remote(own.at[from_x], wide.at[to_x, pl.ds(0, CY)], ss.at[0], rs.at[0], at(a, b, 0)).start()
            elif b == -1:
                remote(own.at[from_x, pl.ds(0, 8)], y_plus.at[to_x], ss.at[1], rs.at[1], at(a, b, 0)).start()
            else:
                remote(own.at[from_x, pl.ds(8, 8)], y_minus.at[to_x], ss.at[2], rs.at[2], at(a, b, 0)).start()
        if ready is None:
            pack[...] = faces(own)
        for a in (-1, 1, 0):
            for b in (-1, 1, 0):
                i = (1 - a) * 3 + 1 - b
                remote(pack, plus.at[i], ss.at[3], rs.at[3], at(a, b, -1)).start()
                remote(pack, minus.at[i], ss.at[4], rs.at[4], at(a, b, 1)).start()

    def exchanged(wide, plus, minus, y_plus, y_minus, ss, rs):
        x_part = wide.at[pl.ds(8, 8), pl.ds(0, CY)]
        return [
            remote(v, v, ss.at[i], rs.at[i], at(1, 0, 0))
            for i, v in enumerate((x_part, y_plus, y_minus, plus, minus))
        ]


    def place(k):
        return 2 * k - 1 if k <= NX // 2 else 2 * NX - 2 * k

    def send_rows(ks):
        for k in ks:
            if k:
                remote(dsend.at[place(k)], dheld.at[place(k)], ds1, dr1, at(k, 0, 0)).start()
        for k, j, _ in group(ks):
            q, i = place(k) if k else 0, int(j > 0)
            remote(send.at[q, j], rows.at[j, q], s1.at[i], r1.at[i], at(k, j, 0)).start()

    send_rows(FAR + CLOSE + [0])

    d_along = remote(dsend.at[pl.ds(1, NX - 1)], dheld.at[pl.ds(1, NX - 1)], ds1, dr1, at(1, 0, 0))
    d_along.wait_recv()
    for j in range(1, NY):
        remote(dheld, dtable.at[j], ds2, dr2, at(0, j, 0)).start()

    d_across = remote(dtable.at[pl.ds(1, NY - 1)], dtable.at[pl.ds(1, NY - 1)], ds2, dr2, at(0, 1, 0))
    d_across.wait_recv()
    dtable[0] = dheld[...]
    exchange(hown, hm, ha_plus, ha_minus, hy_plus, hy_minus, hpack, hs, hr, ready=True)
    hm[0:CX, 0:CY, :] = hown[...]
    places = dtable[...].reshape(NY * NX, 128)
    own_lanes = iota((NY * NX, 128), 1) // CAP == iota((NY * NX, 128), 0) // NX
    places = jnp.where(own_lanes, places, 0.0).astype(BF16)
    cell = (iota((CX * CY, 128), 0) + 1).astype(F32)
    landing = []
    for c in range(CAP):
        lanes = (iota((CX * CY, 128), 1) % CAP == c).astype(F32).astype(BF16)
        landing.append((dot_nt(lanes, places) == cell).astype(F32).astype(BF16))
    landing = jnp.concatenate(landing, axis=1)

    came = [
        remote(rows.at[0, pl.ds(1, NX - 1)], rows.at[0, pl.ds(1, NX - 1)], s1.at[0], r1.at[0], at(1, 0, 0)),
        remote(rows.at[pl.ds(1, NY - 1)], rows.at[pl.ds(1, NY - 1)], s1.at[1], r1.at[1], at(0, 1, 0)),
    ]
    for w in came:
        w.wait_recv()
    arrived = jnp.concatenate([rows[:, :, c, :].reshape(NY * NX, CZ) for c in range(CAP)], axis=0)
    added[...] = picked(landing, three(arrived)).reshape(CX, CY, CZ)
    loads[2].wait()
    prior[...] = prior[...] + added[...]

    exchange(prior, xm, xa_plus, xa_minus, xy_plus, xy_minus, xpack, xs_, xr)
    xm[0:CX, 0:CY, :] = prior[...]

    h_waits = exchanged(hm, ha_plus, ha_minus, hy_plus, hy_minus, hs, hr)
    for w in h_waits:
        w.wait_recv()
    spread_faces(ha_plus, ha_minus, ha)
    upper = iota((EX, 8, CZ), 1) < 4
    hm[:, CY:EY, :] = jnp.where(upper, hy_plus[...], hy_minus[...])

    def inside(i, n):
        return (i < n - 1).astype(F32), (i > 0).astype(F32)

    (x_hi, x_lo), (y_hi, y_lo), (z_hi, z_lo) = inside(gx, NX), inside(gy, NY), inside(gz, NZ)
    row = iota((EY, CZ), 0)
    y_mask = jnp.where(row < CY, 1.0, jnp.where(row < CY + 4, y_hi, y_lo))
    z_mask = jnp.where(iota((EY, CZ), 1) < CZ // 2, z_hi, z_lo)
    for xp in range(EX):
        scale = y_mask if xp < CX else y_mask * (x_hi if xp < 12 else x_lo)
        h0 = hm[xp] * scale
        h1 = ha[xp] * (scale * z_mask)
        hm[xp] = h0
        ha[xp] = h1
        em[xp] = h0 * h0 / (1.0 + 10.5 * h0)
        ea[xp] = h1 * h1 / (1.0 + 10.5 * h1)

    x_waits = exchanged(xm, xa_plus, xa_minus, xy_plus, xy_minus, xs_, xr)
    for w in x_waits:
        w.wait_recv()
    spread_faces(xa_plus, xa_minus, xa)
    xm[:, CY:EY, :] = jnp.where(upper, xy_plus[...], xy_minus[...])

    def cells(width):
        return list(range(CX + width)) + list(range(EX - width, EX))

    def filtered(m, a, width):
        t = {x: smooth_zy(m[x], a[x]) for x in cells(width + 1)}
        out = {}
        for x in cells(width):
            lo, mid, hi = t[(x - 1) % EX], t[x], t[(x + 1) % EX]
            out[x] = tuple(mid[i] + 0.5 * (lo[i] + hi[i]) for i in range(2))
        return out

    m = {x: xm[x] * hm[x] for x in range(EX)}
    a = {x: xa[x] * ha[x] for x in range(EX)}
    us, gs = [], []
    for step in range(4):
        width = 3 - step
        t = filtered(m, a, width)
        um, ua = {}, {}
        for x in cells(width):
            um[x] = t[x][0] - m[x]
            ua[x] = t[x][1] - a[x]
            if step == 0:
                um[x] = um[x] - 10.5 * xm[x]
                ua[x] = ua[x] - 10.5 * xa[x]
        m = {x: em[x] * um[x] for x in cells(width)}
        a = {x: ea[x] * ua[x] for x in cells(width)}
        us.append([um[x][0:CY] for x in range(CX)])
        gs.append([m[x][0:CY] for x in range(CX)])

    us = [[halves(u) + (u,) for u in v] for v in us]
    gs_s = [[halves(g) + (g,) for g in v] for v in gs[:3]]
    row8 = iota((8, CZ), 0)
    lane8 = iota((8, CZ), 1)

    def pair_add(p, q):
        s, e = two_sum(p[0], q[0])
        return s, e + (p[1] + q[1])

    high, rest = jnp.zeros((8, CZ), F32), jnp.zeros((8, CZ), F32)
    for k, (i, j) in enumerate(((0, 0), (0, 1), (1, 1), (1, 2), (2, 2), (2, 3))):
        terms = []
        for x in range(CX):
            p, e = two_prod(gs_s[i][x][2], us[j][x][2], gs_s[i][x][:2], us[j][x][:2])
            terms += [(p[0:8], e[0:8]), (p[8:16], e[8:16])]
        v = tree(terms, pair_add)
        for shift in (4, 2, 1):
            v = pair_add(v, tuple(pltpu.roll(w, shift, 0) for w in v))
        high, rest = jnp.where(row8 == k, v[0], high), jnp.where(row8 == k, v[1], rest)
    v = high, rest
    for shift in (64, 32, 16, 8, 4, 2, 1):
        v = pair_add(v, tuple(pltpu.roll(w, shift, 1) for w in v))
    v = jnp.where(lane8 == row8, v[0], jnp.where(lane8 == row8 + 64, v[1], 0.0))
    part_a[0] = jnp.sum(v, axis=0, keepdims=True)

    def all_of(buf, n):
        v = buf[...].reshape(n, CZ)
        v = tree([(v[8 * i : 8 * i + 8], jnp.zeros((8, CZ), F32)) for i in range(n // 8)], pair_add)
        for shift in (4, 2, 1):
            v = pair_add(v, tuple(pltpu.roll(w, shift, 0) for w in v))
        v = v[0] + pltpu.roll(jnp.where(lane8 < 64, v[1], 0.0), 64, 1)
        return v[0:1]

    for l in (2, 1, 3, 0):
        for j in (4, 3, 5, 2, 6, 1, 7, 0):
            if j or l:
                remote(part_a.at[0], part_a.at[j * NZ + l], as_, ar, at(0, j, l)).start()
    a_all = remote(part_a.at[pl.ds(1, NY * NZ - 1)], part_a.at[pl.ds(1, NY * NZ - 1)], as_, ar, at(0, 1, 0))
    a_all.wait_recv()
    part_b[0] = all_of(part_a, NY * NZ)
    for k in FAR + CLOSE:
        remote(part_b.at[0], part_b.at[k], bs, br, at(k, 0, 0)).start()
    b_all = remote(part_b.at[pl.ds(1, NX - 1)], part_b.at[pl.ds(1, NX - 1)], bs, br, at(1, 0, 0))
    b_all.wait_recv()
    s = all_of(part_b, NX)
    moments = [quick_sum(s[:, k : k + 1], s[:, 64 + k : 65 + k]) for k in range(6)]

    xs, rs = coefficients(moments)
    xs = [jnp.broadcast_to(c, (CY, CZ)) for c in xs]
    rs = [jnp.broadcast_to(c, (CY, CZ)) for c in rs]
    for x in range(CX):
        t_buf[x] = xs[0] * gs[0][x] + xs[1] * gs[1][x] + xs[2] * gs[2][x]
        r_buf[x] = (rs[0] * gs[0][x] + rs[1] * gs[1][x]) + (rs[2] * gs[2][x] + rs[3] * gs[3][x])
    for w in [d_along] + came + h_waits + x_waits + [a_all, b_all]:
        w.wait_send()
    for j in range(1, NY):
        remote(dheld, dtable.at[j], ds2, dr2, at(0, j, 0)).wait_send()


def local(prior, h, heat, owner, dest):
    n = dest.shape[0]
    vmem = pl.BlockSpec(memory_space=pltpu.VMEM)
    hbm = pl.BlockSpec(memory_space=pltpu.HBM)
    block = jax.ShapeDtypeStruct((CX, CY, CZ), F32)
    V = lambda *shape: pltpu.VMEM(shape, F32)
    D = pltpu.SemaphoreType.DMA
    wide = V(EX, EY, CZ)
    nine, ys, tile = V(9, 8, CZ), V(EX, 8, CZ), V(8, CZ)
    own = V(CX, CY, CZ)
    scratch = [
        own, pltpu.VMEM((1, n), jnp.int32), pltpu.VMEM((1, n), jnp.int32), V(n, CZ), own, wide, wide, wide, nine, nine, wide, nine, nine,
        ys, ys, ys, ys, tile, tile, wide, wide,
        V(NX, NY, CAP, CZ), V(NY, NX, CAP, CZ),
        V(NX, 1, 128), V(NX, 1, 128), V(NY, NX, 1, 128),
        V(NY * NZ, 1, CZ), V(NX, 1, CZ),
        D((5,)), D((2,)), D((2,)), D, D, D, D,
        D((5,)), D((5,)), D((5,)), D((5,)), D, D, D, D,
    ]
    step, rest, added = pl.pallas_call(
        kernel,
        out_shape=(block, block, block),
        in_specs=[hbm] * 5,
        out_specs=(vmem,) * 3,
        scratch_shapes=scratch,
        compiler_params=pltpu.CompilerParams(
            collective_id=0, has_side_effects=True, vmem_limit_bytes=VMEM_BYTES
        ),
    )(owner.reshape(1, n), dest.reshape(1, n), prior, h, heat)
    deposited = prior + added
    over = 1.0 / h
    return deposited + step * over, rest * (over + 10.5), deposited


def solution(mesh):
    placed = (
        P("gx", "gy", "gz"),
        P("gx", "gy", "gz"),
        P(("gx", "gy"), "gz"),
        P(("gx", "gy"), None),
        P(("gx", "gy")),
    )
    return jax.shard_map(
        local,
        mesh=mesh,
        in_specs=placed,
        out_specs=(P("gx", "gy", "gz"), P("gx", "gy", "gz"), P("gx", "gy", "gz")),
        check_vma=False,
    )
```
